256 devices in a mesh: dp: 16 (over y_lo, z), shard: 16 (over x, y_hi, core).
Axes of the slice: x: 4, y: 4 (y_hi: 2, y_lo: 2; y = y_hi * 2 + y_lo), z: 8, core: 2. Of those that a mesh axis runs over, the one named last changes fastest.
Arguments:
- train_ids: int32 [4096], P('dp'), may hold values from 0 to 31999, as said below
- query_ids: int32 [2048], P('dp'), may hold values from 0 to 31999, as said below
- embed: bfloat16 [32000, 2048], P('shard'), as said below
- norm_gain: float32 [2048], replicated, may hold values from 0.1 to 1.9
- w_gate: bfloat16 [2048, 5504], P(None, 'shard'), may hold values from -0.125 to 0.125
- w_up: bfloat16 [2048, 5504], P(None, 'shard'), may hold values from -0.125 to 0.125
- cotangent: bfloat16 [2048, 2048], P('dp'), as said below
Outputs:
- solution: float32 [5504, 2048], P('shard', 'dp')
The draws below stay inside these ranges and needn't reach their ends.
Inputs may be any that keep to these rules, and one draw needn't show every extreme that they name: `train_ids`: token ids of the vocabulary. `query_ids`: token ids of the vocabulary. `embed`: real values, drawn afresh for every entry. `cotangent`: real values, drawn afresh for every entry.
All inputs are finite; a program needn't handle non-finite values.
Results may differ from the reference program's by a relative error of at most 0.0061.
Values may be sent and summed in bfloat16 or wider, within the bound.
No kernel may reach another device: no remote copies, remote signals or barrier semaphores. Data moves between devices by JAX's collectives and lax.ppermute only.
A program may use at most 64 MiB of HBM per device.

```python
import math
import jax
import jax.numpy as jnp
from jax import lax

D = 2048
F = 5504
V = 32000
TOK_DP = 256
QLEN = 2048
ITERS = 3
TOKENS = 4096


def id_pools(key):
    group_count = TOKENS // TOK_DP
    return jax.random.randint(jax.random.fold_in(key, 101), (group_count, 16), 0, V).astype(jnp.int32)


def mixed_ids(key, pools, count):
    group_count = pools.shape[0]
    pick_key, free_key, coin_key = jax.random.split(key, 3)
    group = jnp.arange(count, dtype=jnp.int32) * group_count // count
    slot = jax.random.randint(pick_key, (count,), 0, pools.shape[1])
    pooled = pools[group, slot]
    free_ids = jax.random.randint(free_key, (count,), 0, V).astype(jnp.int32)
    coin = jax.random.randint(coin_key, (count,), 0, 2)
    chosen = jnp.where(coin == 1, pooled, free_ids).astype(jnp.int32)
    chosen = chosen.at[0].set(0)
    chosen = chosen.at[count - 1].set(V - 1)
    return chosen


def draw_train_ids(key, part):
    pools = id_pools(key)
    key = jax.random.fold_in(key, 3)
    return mixed_ids(key, pools, TOKENS)


def draw_query_ids(key, part):
    pools = id_pools(key)
    key = jax.random.fold_in(key, 5)
    return mixed_ids(key, pools, QLEN)


def draw_embed(key, part):
    key = jax.random.fold_in(key, 7)
    base_key, row_key, col_key = jax.random.split(key, 3)
    row_scale = jnp.exp(jax.random.uniform(row_key, (V, 1), jnp.float32, 0.0, math.log(10.0)))
    col_scale = jnp.exp(jax.random.uniform(col_key, (1, D), jnp.float32, 0.0, math.log(10.0)))
    base_vals = jnp.clip(jax.random.normal(base_key, (V, D), jnp.float32), -5.0, 5.0)
    return (0.1 * base_vals * row_scale * col_scale).astype(jnp.bfloat16)


def block_emphasis(key, strong, weak):
    group_count = TOKENS // TOK_DP
    offset = jax.random.randint(key, (), 1, group_count)
    row_group = jnp.arange(QLEN, dtype=jnp.int32) * group_count // QLEN
    col_group = jnp.arange(D, dtype=jnp.int32) * group_count // D
    target = (row_group + offset) % group_count
    return jnp.where(target[:, None] == col_group[None, :], strong, weak).astype(jnp.float32)


def draw_cotangent(key, part):
    key = jax.random.fold_in(key, 13)
    base_key, col_key, block_key = jax.random.split(key, 3)
    position = jnp.arange(D, dtype=jnp.float32) / (D - 1)
    jitter = jnp.exp(jax.random.uniform(col_key, (1, D), jnp.float32, -0.3, 0.3))
    base_vals = jnp.clip(jax.random.normal(base_key, (QLEN, D), jnp.float32), -5.0, 5.0)
    rise_scale = jnp.exp(position * math.log(3.0))
    emphasis = block_emphasis(block_key, 4.0, 0.5)
    return (base_vals * rise_scale[None, :] * jitter * emphasis).astype(jnp.bfloat16)


def block_levels(key, extent, cuts, least, high):
    factor_of = 1.0
    for dim, blocks in cuts:
        heights = jax.random.uniform(jax.random.fold_in(jax.random.fold_in(key, 6), dim), (blocks,), jnp.float32, least / len(cuts), high / len(cuts))
        factor_of = factor_of * jnp.repeat(jnp.exp(heights), extent[dim] // blocks).reshape((-1,) + (1,) * (len(extent) - 1 - dim))
    return factor_of


def centred(key, extent, width, reach, cuts=(), kind=jnp.bfloat16):
    level = block_levels(key, extent, cuts, -0.22, 0.18) if cuts else 1.0
    drawn = jax.random.normal(key, extent, jnp.float32) * width * level
    return jnp.minimum(jnp.maximum(drawn, -reach), reach).astype(kind)


def setup_inputs(seed: int = 0) -> dict:
    key_of = jax.random.split(jax.random.key(seed), 8)
    return {
        "train_ids": draw_train_ids(jax.random.fold_in(key_of[7], 71), 0),
        "query_ids": draw_query_ids(jax.random.fold_in(key_of[7], 71), 0),
        "embed": draw_embed(jax.random.fold_in(key_of[7], 71), 0),
        "norm_gain": jnp.clip(1.0 + 0.18 * jax.random.normal(key_of[3], (D,), jnp.float32), 0.1, 1.9),
        "w_gate": centred(key_of[4], (D, F), D ** -0.5, 0.125, ((1, 16),)),
        "w_up": centred(key_of[5], (D, F), D ** -0.5, 0.125, ((1, 16),)),
        "cotangent": draw_cotangent(jax.random.fold_in(key_of[7], 71), 0),
    }


norm_eps = 1e-05
damping = 0.1

def hidden_acts(rows, norm_gain, w_gate, w_up):
    values = rows.astype(jnp.float32)
    inv_scale = lax.rsqrt(lax.optimization_barrier(jnp.mean(values * values, axis=-1, keepdims=True)) + norm_eps)
    normed = (values * inv_scale * norm_gain.astype(jnp.float32)).astype(jnp.bfloat16)
    gate_out = jnp.dot(normed, w_gate, preferred_element_type=jnp.float32)
    upward = jnp.dot(normed, w_up, preferred_element_type=jnp.float32)
    return (jax.nn.silu(gate_out) * upward).astype(jnp.bfloat16)

def reference(train_ids, query_ids, embed, norm_gain, w_gate, w_up, cotangent):
    rows = jnp.take(embed, train_ids, axis=0)
    query_rows = jnp.take(embed, query_ids, axis=0)
    hidden_vals = hidden_acts(rows, norm_gain, w_gate, w_up)
    query_vals = hidden_acts(query_rows, norm_gain, w_gate, w_up)
    target_vec = jnp.dot(query_vals.T, cotangent, preferred_element_type=jnp.float32) / math.sqrt(QLEN)

    def apply_ggn(vector):
        tangent = jnp.dot(hidden_vals, vector.astype(jnp.bfloat16), preferred_element_type=jnp.float32).astype(jnp.bfloat16)
        return jnp.dot(hidden_vals.T, tangent, preferred_element_type=jnp.float32) / TOKENS + damping * vector
    solution = jnp.zeros_like(target_vec)
    residual = target_vec
    direction = target_vec
    norm_now = jnp.sum(residual * residual)
    for turn_index in range(ITERS):
        curved = apply_ggn(direction)
        step_size = norm_now / jnp.sum(direction * curved)
        solution = solution + step_size * direction
        residual = residual - step_size * curved
        norm_next = jnp.sum(residual * residual)
        direction = residual + norm_next / norm_now * direction
        norm_now = norm_next
    return solution
```

```python
import math

import jax
import jax.numpy as jnp
from jax import lax
from jax.sharding import PartitionSpec as P

norm_eps = 1e-05
damping = 0.1

bf16 = jnp.bfloat16
f32 = jnp.float32

CHIPS = [[c + 2 * i for i in range(8)] for c in range(2)]
CORE = [(i, i ^ 1) for i in range(16)]
YLO = [(i, i ^ 8) for i in range(16)]


def z_shift(step):
    return [(i, (i & 8) | ((i + step) & 7)) for i in range(16)]


def swap_core(v):
    return lax.ppermute(v, "shard", CORE)


def scatter_chips(v):
    return lax.all_to_all(v, "shard", 0, 0, axis_index_groups=CHIPS, tiled=True)


def share_chips(v):
    spread = jnp.broadcast_to(v[None], (8,) + v.shape)
    return lax.all_to_all(spread, "shard", 0, 0, axis_index_groups=CHIPS, tiled=True)


def split3(v):
    hi = v.astype(bf16).astype(f32)
    mid = (v - hi).astype(bf16).astype(f32)
    low = v - hi - mid
    return jnp.stack([hi, mid, low]).astype(bf16)


def guarded(top, bottom):
    fine = bottom > 0
    return jnp.where(fine, top / jnp.where(fine, bottom, 1.0), 0.0)


def dot_t(a, b):
    return lax.dot_general(a, b, (((0,), (0,)), ((), ())), preferred_element_type=f32)


def dot(a, b):
    return jnp.dot(a, b, preferred_element_type=f32)


def embedding_rows(train_ids, query_ids, embed, core):
    height = embed.shape[0]
    ids = jnp.concatenate([train_ids.reshape(2, -1), query_ids.reshape(2, -1)], axis=1)
    ids = jnp.where(core == 0, ids, ids[::-1])
    offset = ids - lax.axis_index("shard") * height
    inside = (offset >= 0) & (offset < height)
    picked = jnp.take(embed, jnp.clip(offset, 0, height - 1).reshape(-1), axis=0)
    picked = jnp.where(inside.reshape(-1)[:, None], picked, jnp.zeros_like(picked))
    half = picked.shape[0] // 2
    other = swap_core(picked[half:])
    mine = picked[:half] + other
    parts = scatter_chips(mine.reshape(8, half // 8, -1))
    return jnp.sum(parts.astype(f32), axis=0)


def normalise(rows, norm_gain):
    inv_scale = lax.rsqrt(jnp.mean(rows * rows, axis=-1, keepdims=True) + norm_eps)
    return (rows * inv_scale * norm_gain).astype(bf16)


def hidden_transposed(normed, w_gate, w_up):
    def product(w):
        return lax.dot_general(w, normed, (((0,), (1,)), ((), ())), preferred_element_type=f32)

    return (jax.nn.silu(product(w_gate)) * product(w_up)).astype(bf16)


def gather_groups(own):
    pair = jnp.stack([own, lax.ppermute(own, "dp", YLO)])
    ups, downs = [pair], [pair]
    for _ in range(3):
        ups.append(lax.ppermute(ups[-1], "dp", z_shift(1)))
        downs.append(lax.ppermute(downs[-1], "dp", z_shift(-1)))
    last_up = lax.ppermute(ups[-1][0], "dp", z_shift(1))
    last_down = lax.ppermute(downs[-1][1], "dp", z_shift(-1))
    blocks = [pair[0], pair[1]]
    for i in range(1, 4):
        blocks += [ups[i][0], ups[i][1], downs[i][0], downs[i][1]]
    return blocks + [last_up, last_down]


def group_order():
    me = lax.axis_index("dp")
    y, z = me // 8, me % 8
    steps = [0]
    for i in range(1, 4):
        steps += [-i, i]
    steps.append(4)
    order = []
    for step in steps:
        for flip in range(2):
            order.append((y ^ flip) * 8 + (z + step) % 8)
    return jnp.stack(order)


def body(train_ids, query_ids, embed, norm_gain, w_gate, w_up, cotangent):
    core = lax.axis_index("shard") % 2
    tokens_total = train_ids.shape[0] * 16
    query_total = query_ids.shape[0] * 16
    units = w_gate.shape[1]
    w_gate_other, w_up_other = swap_core(w_gate), swap_core(w_up)

    with jax.named_scope("rows"):
        rows = embedding_rows(train_ids, query_ids, embed, core)
    with jax.named_scope("normed"):
        normed = normalise(rows, norm_gain)
        normed = share_chips(normed).reshape(-1, rows.shape[1])
    with jax.named_scope("acts"):
        own = hidden_transposed(normed, w_gate, w_up)
        other = hidden_transposed(normed, w_gate_other, w_up_other)
        n_train = train_ids.shape[0] // 2
        package = jnp.concatenate(
            [
                own[:, :n_train],
                other[:, :n_train],
                jnp.concatenate([own[:, n_train:], other[:, n_train:]], axis=1),
            ],
            axis=0,
        )
    with jax.named_scope("groups"):
        blocks = gather_groups(package)
        acts = jnp.concatenate([b[: 2 * units] for b in blocks], axis=1)
        query = jnp.concatenate([b[2 * units :] for b in blocks], axis=1)
    with jax.named_scope("cotangent"):
        n_query = query_ids.shape[0] // 2
        mine = lax.dynamic_slice_in_dim(cotangent, core * n_query, n_query, axis=0)
        columns = lax.all_to_all(
            mine.reshape(n_query, 16, -1).transpose(1, 0, 2), "dp", 0, 0, tiled=True
        )
        columns = jnp.take(columns, group_order(), axis=0)
        empty = jnp.zeros_like(columns)
        wide = jnp.concatenate(
            [
                jnp.concatenate([columns, empty], axis=2),
                jnp.concatenate([empty, columns], axis=2),
            ],
            axis=1,
        ).reshape(-1, 2 * columns.shape[2])

    def across_cores(pair):
        return pair + swap_core(pair[::-1])

    with jax.named_scope("rhs"):
        part = dot(query, wide)
        width = part.shape[1] // 2
        part = jnp.stack([part[:, :width], part[:, width:]]) / math.sqrt(query_total)
        residual = across_cores(part)

    def scattered_tangent(res):
        partial = dot_t(acts, res.reshape(-1, width).astype(bf16)).astype(bf16)
        parts = scatter_chips(partial.reshape(8, -1, width))
        return jnp.sum(parts.astype(f32), axis=0)

    def shared_tangent(block, scalars):
        extra = split3(scalars)
        extra = jnp.pad(extra, ((0, 16 - extra.shape[0]), (0, width - extra.shape[1])))
        message = jnp.concatenate([block.astype(bf16), extra], axis=0)
        got = share_chips(message).reshape(8, -1, width)
        rows = block.shape[0]
        sums = jnp.sum(got[:, rows : rows + 3, : scalars.shape[0]].astype(f32), axis=(0, 1))
        return got[:, :rows].reshape(-1, width), sums

    def curved_product(tangent):
        return across_cores(dot(acts, tangent).reshape(2, -1, width)) / tokens_total

    with jax.named_scope("first"):
        r0 = residual
        block0 = scattered_tangent(r0)
        block0 = block0.astype(bf16).astype(f32)
        t0, sums = shared_tangent(block0, jnp.stack([jnp.sum(r0 * r0), jnp.sum(block0 * block0)]))
        rr0, tt0 = sums[0], sums[1]
        tt0 = tt0 + swap_core(tt0)
        pp0 = rr0
        inv_alpha0 = guarded(tt0 / tokens_total + damping * pp0, rr0)
        alpha0 = guarded(1.0, inv_alpha0)
        p0 = r0
        r1 = r0 - alpha0 * (curved_product(t0) + damping * p0)
    with jax.named_scope("second"):
        block1 = scattered_tangent(r1)
        block1 = block1.astype(bf16).astype(f32)
        w1, sums = shared_tangent(
            block1,
            jnp.stack([jnp.sum(r1 * r1), jnp.sum(block1 * block1), jnp.sum(block1 * block0)]),
        )
        rr1 = sums[0]
        cross = sums[1:]
        cross = cross + swap_core(cross)
        beta0 = guarded(rr1, rr0)
        tt1 = cross[0] + 2 * beta0 * cross[1] + beta0 * beta0 * tt0
        pp1 = rr1 + beta0 * beta0 * pp0
        inv_alpha1 = guarded(tt1 / tokens_total + damping * pp1, rr1)
        alpha1 = guarded(1.0, inv_alpha1)
        t1 = (w1.astype(f32) + beta0 * t0.astype(f32)).astype(bf16)
        p1 = r1 + beta0 * p0
        r2 = r1 - alpha1 * (curved_product(t1) + damping * p1)
    with jax.named_scope("third"):
        block2 = scattered_tangent(r2)
        step1 = block1 + beta0 * block0
        partials = jnp.stack(
            [0.5 * jnp.sum(r2 * r2), jnp.sum(block2 * block2), jnp.sum(block2 * step1)]
        )
        got = lax.all_to_all(jnp.broadcast_to(partials[None], (16, 3)), "shard", 0, 0, tiled=True)
        sums = jnp.sum(got, axis=0)
        rr2 = sums[0]
        beta1 = guarded(rr2, rr1)
        tt2 = sums[1] + 2 * beta1 * sums[2] + beta1 * beta1 * tt1
        pp2 = rr2 + beta1 * beta1 * pp1
        inv_alpha2 = guarded(tt2 / tokens_total + damping * pp2, rr2)

    with jax.named_scope("whole"):
        mine = jnp.stack([rr0, rr1, rr2, inv_alpha0, inv_alpha1, inv_alpha2, beta0, beta1])
        every = lax.all_to_all(jnp.broadcast_to(mine[None], (16, 8)), "dp", 0, 0, tiled=True)
        norms = every[:, 0:3]
        ia0, ia1, ia2 = every[:, 3], every[:, 4], every[:, 5]
        b0, b1 = every[:, 6], every[:, 7]

        def apply_whole(u):
            u0, u1, u2 = u[:, 0], u[:, 1], u[:, 2]
            s2 = u2
            s1 = u1 - b1 * s2
            s0 = u0 - b0 * u1
            return jnp.stack([s0 * ia0, s1 * ia1 - s0 * ia0, s2 * ia2 - s1 * ia1], axis=1)

        def inner(u, v):
            return jnp.sum(u * v * norms)

        answer = jnp.zeros_like(norms)
        res = jnp.concatenate([jnp.ones_like(norms[:, :1]), jnp.zeros_like(norms[:, :2])], axis=1)
        direction = res
        norm_now = inner(res, res)
        for turn in range(3):
            curved = apply_whole(direction)
            step = norm_now / inner(direction, curved)
            answer = answer + step * direction
            if turn < 2:
                res = res - step * curved
                norm_next = inner(res, res)
                direction = res + norm_next / norm_now * direction
                norm_now = norm_next
        mix = lax.dynamic_slice_in_dim(answer, lax.axis_index("dp"), 1, axis=0)[0]
        return mix[0] * r0[0] + mix[1] * r1[0] + mix[2] * r2[0]


def solution(mesh):
    placed = (
        P("dp"),
        P("dp"),
        P("shard", None),
        P(),
        P(None, "shard"),
        P(None, "shard"),
        P("dp", None),
    )
    return jax.shard_map(
        body, mesh=mesh, in_specs=placed, out_specs=P("shard", "dp"), check_vma=False
    )
```

```python
import functools
import math

import jax
import jax.numpy as jnp
from jax import lax
from jax.experimental import pallas as pl
from jax.experimental.pallas import tpu as pltpu
from jax.sharding import PartitionSpec as P

norm_eps = 1e-05
damping = 0.1

bf16 = jnp.bfloat16
f32 = jnp.float32

CHIPS = [[c + 2 * i for i in range(8)] for c in range(2)]
CORE = [(i, i ^ 1) for i in range(16)]
YLO = [(i, i ^ 8) for i in range(16)]
VMEM = pl.BlockSpec(memory_space=pltpu.VMEM)
SMEM = pl.BlockSpec(memory_space=pltpu.SMEM)
UNITS = 344
BOTH = 2 * UNITS
PACK = 1040
TOKENS = 4096
HALF = TOKENS // 2


def z_shift(step):
    return [(i, (i & 8) | ((i + step) & 7)) for i in range(16)]


def swap_core(v):
    return lax.ppermute(v, "shard", CORE)


def exchange_chips(v):
    return lax.all_to_all(v, "shard", 0, 0, axis_index_groups=CHIPS, tiled=True)


def local_call(kernel, outs, *args, specs=None, **more):
    return pl.pallas_call(
        kernel,
        out_shape=outs,
        in_specs=specs or [VMEM] * len(args),
        out_specs=jax.tree.map(lambda _: VMEM, outs),
        compiler_params=pltpu.CompilerParams(vmem_limit_bytes=48 * 2**20),
        **more,
    )(*args)


def shape(dims, dtype):
    return jax.ShapeDtypeStruct(dims, dtype)


def guarded(top, bottom):
    fine = bottom > 0
    return jnp.where(fine, top / jnp.where(fine, bottom, 1.0), 0.0)


def dot(a, b):
    return jnp.dot(a, b, preferred_element_type=f32)


def total(v):
    return jnp.sum(v, axis=(0, 1), keepdims=True)


def lanes(values, dims):
    lane = lax.broadcasted_iota(jnp.int32, dims, 1)
    row = lax.broadcasted_iota(jnp.int32, dims, 0)
    out = jnp.zeros(dims, f32)
    for i, v in enumerate(values):
        out = jnp.where((lane == i) & (row == 0), v, out)
    return out


def lookup_kernel(place, train, query, table, mine, other, hot):
    height = table.shape[0]

    @pl.when(pl.program_id(0) == 0)
    def _():
        core, shard = place[0], place[1]

        def column(row):
            return jnp.broadcast_to(row, (128, 128)).T

        own_train = column(train[pl.ds(core, 1), :])
        other_train = column(train[pl.ds(1 - core, 1), :])
        asked = column(query[...])
        first = core == 0
        own_query = jnp.where(first, asked[:64], asked[64:])
        other_query = jnp.where(first, asked[64:], asked[:64])
        ids = jnp.concatenate([own_train, own_query, other_train, other_query], axis=0)
        ids = ids - shard * height
        lane = lax.broadcasted_iota(jnp.int32, ids.shape, 1)
        for start in range(0, height, 128):
            wide = min(128, height - start)
            hit = jnp.where(ids == lane + start, 1.0, 0.0).astype(bf16)
            hot[:, start : start + wide] = hit[:, :wide]

    found = dot(hot[...], table[...]).astype(bf16)
    mine[...] = found[:192]
    other[...] = found[192:]


def lookup(train_ids, query_ids, embed, core):
    height, wide = embed.shape
    step = 256
    place = jnp.stack([core, lax.axis_index("shard")])
    out = shape((192, wide), bf16)
    return pl.pallas_call(
        lookup_kernel,
        grid=(wide // step,),
        out_shape=(out, out),
        in_specs=[SMEM, VMEM, VMEM, pl.BlockSpec((height, step), lambda j: (0, j))],
        out_specs=[pl.BlockSpec((192, step), lambda j: (0, j))] * 2,
        scratch_shapes=[pltpu.VMEM((384, height), bf16)],
        compiler_params=pltpu.CompilerParams(vmem_limit_bytes=48 * 2**20),
    )(place, train_ids.reshape(2, 128), query_ids.reshape(1, 128), embed)


def norm_kernel(parts, gain, out):
    rows = jnp.sum(parts[...].astype(f32), axis=0)
    inv_scale = lax.rsqrt(jnp.mean(rows * rows, axis=-1, keepdims=True) + norm_eps)
    normed = (rows * inv_scale * gain[...]).astype(bf16)
    for i in range(8):
        out[i] = normed


def acts_kernel(normed, w_gate, w_up, w_gate_other, w_up_other, out):
    rows = normed[...]

    def hidden(gate_w, up_w):
        gate = dot(rows, gate_w[...])
        return (gate / (1.0 + jnp.exp(-gate))) * dot(rows, up_w[...])

    own = hidden(w_gate, w_up)
    other = hidden(w_gate_other, w_up_other)
    asked = jnp.concatenate([own[128:], other[128:]], axis=0)
    fill = jnp.zeros((PACK - 3 * UNITS, 128), f32)
    out[...] = jnp.concatenate([own[:128].T, other[:128].T, asked.T, fill], axis=0).astype(bf16)


def gather_groups(own):
    partner = lax.ppermute(own, "dp", YLO)
    pair = jnp.stack([own, partner])
    ups, downs = [pair], [pair]
    for _ in range(3):
        ups.append(lax.ppermute(ups[-1], "dp", z_shift(1)))
        downs.append(lax.ppermute(downs[-1], "dp", z_shift(-1)))
    last_up = lax.ppermute(ups[-1][0], "dp", z_shift(1))
    last_down = lax.ppermute(downs[-1][1], "dp", z_shift(-1))
    return pair, [pair] + [b for i in range(1, 4) for b in (ups[i], downs[i])], [last_up, last_down]


def group_order():
    me = lax.axis_index("dp")
    y, z = me // 8, me % 8
    order = []
    for step in (0, -1, 1, -2, 2, -3, 3, 4):
        for flip in range(2):
            order.append((y ^ flip) * 8 + (z + step) % 8)
    return jnp.stack(order)


def rhs_kernel(scale, *refs):
    pairs, singles, wide, part, flip, acts = refs[:7], refs[7:9], refs[9], refs[10], refs[11], refs[12]
    blocks = [(p, i) for p in pairs for i in range(2)]
    out = jnp.zeros((PACK - BOTH, 256), f32)
    for b in range(16):
        block = blocks[b][0][blocks[b][1]] if b < 14 else singles[b - 14][...]
        acts[:, b * 128 : (b + 1) * 128] = block[:BOTH]
        out = out + dot(block[BOTH:], wide[b])
    out = out * scale
    part[:UNITS] = out[:UNITS, :128]
    part[UNITS:] = out[:UNITS, 128:]
    flip[:UNITS] = out[:UNITS, 128:]
    flip[UNITS:] = out[:UNITS, :128]


def spread_tangent(res, acts, tangent):
    res_t = res.T.astype(bf16)
    for i in range(8):
        tangent[i] = dot(res_t, acts[:, i * 256 : (i + 1) * 256]).astype(bf16)


def first_kernel(part, got, acts, res_out, sums, tangent):
    res = part[...] + got[...]
    res_out[...] = res
    sums[...] = lanes([total(res * res)], (8, 128))
    spread_tangent(res, acts, tangent)


def share_kernel(parts, sums, *refs):
    earlier, (block_out, message) = refs[:-2], refs[-2:]
    block = jnp.sum(parts[...].astype(f32), axis=0).astype(bf16)
    block_out[...] = block
    block = block.astype(f32)
    values = [sums[0:1, 0:1], total(block * block)]
    if earlier:
        values.append(total(block * earlier[0][...].astype(f32)))
    extra = lanes(values, (16, 256))
    hi = extra.astype(bf16).astype(f32)
    mid = (extra - hi).astype(bf16).astype(f32)
    low = extra - hi - mid
    row = lax.broadcasted_iota(jnp.int32, (16, 256), 0)
    first_row = jnp.where(row == 0, hi, 0.0)
    mid = jnp.broadcast_to(mid[0:1], (16, 256))
    low = jnp.broadcast_to(low[0:1], (16, 256))
    extra = jnp.where(row == 1, mid, jnp.where(row == 2, low, first_row))
    whole = jnp.concatenate([block, extra], axis=0).astype(bf16)
    for i in range(8):
        message[i] = whole


def curve_kernel(got, acts, *refs):
    if len(refs) == 4:
        tangent_out, part, flip, sums_out = refs
    else:
        past, state, part, flip, sums_out = refs
    extra = got[0, 128:144, :].astype(f32)
    for i in range(1, 8):
        extra = extra + got[i, 128:144, :].astype(f32)
    sums = jnp.sum(extra, axis=0, keepdims=True)[:, :128]
    if len(refs) == 5:
        beta = guarded(sums[:, 0:1], state[0:1, 1:2])
    out = jnp.zeros((BOTH, 128), f32)
    for i in range(8):
        tangent = got[i, :128, :]
        if len(refs) == 4:
            tangent_out[i] = tangent
        else:
            tangent = (tangent.astype(f32) + beta * past[i].astype(f32)).astype(bf16)
        out = out + lax.dot_general(
            acts[:, i * 256 : (i + 1) * 256],
            tangent,
            (((1,), (1,)), ((), ())),
            preferred_element_type=f32,
        )
    row = lax.broadcasted_iota(jnp.int32, (8, 128), 0)
    sums = jnp.where(row == 0, jnp.broadcast_to(sums, (8, 128)), 0.0)
    sums_out[...] = sums
    part[...] = out
    flip[:UNITS] = out[UNITS:]
    flip[UNITS:BOTH] = out[:UNITS]
    flip[BOTH:] = sums


def second_kernel(part, got, sums, res, acts, res_out, state, tangent):
    rr = sums[0:1, 0:1]
    tt = sums[0:1, 1:2] + got[BOTH : BOTH + 1, 1:2]
    inv_alpha = guarded(tt / TOKENS + damping * rr, rr)
    alpha = guarded(jnp.ones_like(inv_alpha), inv_alpha)
    old = res[...]
    new = old - alpha * ((part[...] + got[:BOTH]) / TOKENS + damping * old)
    res_out[...] = new
    state[...] = lanes([total(new * new), rr, tt, rr, inv_alpha], (8, 128))
    spread_tangent(new, acts, tangent)


def third_kernel(part, got, sums, past, res, res_before, acts, res_out, state, tangent):
    rr = sums[0:1, 0:1]
    ww = sums[0:1, 1:2] + got[BOTH : BOTH + 1, 1:2]
    cross = sums[0:1, 2:3] + got[BOTH : BOTH + 1, 2:3]
    rr0, tt0, pp0, inv_alpha0 = (past[0:1, i : i + 1] for i in range(1, 5))
    beta = guarded(rr, rr0)
    tt = ww + 2.0 * beta * cross + beta * beta * tt0
    pp = rr + beta * beta * pp0
    inv_alpha = guarded(tt / TOKENS + damping * pp, rr)
    alpha = guarded(jnp.ones_like(inv_alpha), inv_alpha)
    old = res[...]
    direction = old + beta * res_before[...]
    new = old - alpha * ((part[...] + got[:BOTH]) / TOKENS + damping * direction)
    res_out[...] = new
    state[...] = lanes(
        [total(new * new), rr0, rr, tt, pp, inv_alpha0, inv_alpha, beta], (8, 128)
    )
    spread_tangent(new, acts, tangent)


def partial_kernel(parts, state, block0, block1, message):
    block2 = jnp.sum(parts[...].astype(f32), axis=0)
    beta = state[0:1, 7:8]
    step1 = block1[...].astype(f32) + beta * block0[...].astype(f32)
    out = lanes([0.5 * state[0:1, 0:1], total(block2 * block2), total(block2 * step1)], (8, 128))
    for i in range(16):
        message[i] = out


def group_kernel(got, state, message):
    sums = jnp.sum(jnp.sum(got[...], axis=0), axis=0, keepdims=True)
    rr0, rr1, tt1, pp1, inv_alpha0, inv_alpha1, beta0 = (state[0:1, i : i + 1] for i in range(1, 8))
    rr2 = sums[:, 0:1]
    beta1 = guarded(rr2, rr1)
    tt2 = sums[:, 1:2] + 2.0 * beta1 * sums[:, 2:3] + beta1 * beta1 * tt1
    pp2 = rr2 + beta1 * beta1 * pp1
    inv_alpha2 = guarded(tt2 / TOKENS + damping * pp2, rr2)
    out = lanes([rr0, rr1, rr2, inv_alpha0, inv_alpha1, inv_alpha2, beta0, beta1], (8, 128))
    for i in range(16):
        message[i] = out


def whole_kernel(me, got, res0, res1, res2, out):
    every = jnp.sum(got[...], axis=1)
    n0, n1, n2, ia0, ia1, ia2, b0, b1 = (every[:, i : i + 1] for i in range(8))

    def apply_whole(u):
        u0, u1, u2 = u
        s0, s1, s2 = u0 - b0 * u1, u1 - b1 * u2, u2
        return s0 * ia0, s1 * ia1 - s0 * ia0, s2 * ia2 - s1 * ia1

    def inner(u, v):
        terms = u[0] * v[0] * n0 + u[1] * v[1] * n1 + u[2] * v[2] * n2
        return jnp.sum(terms, axis=0, keepdims=True)

    zero = jnp.zeros_like(n0)
    answer = (zero, zero, zero)
    res = (jnp.ones_like(n0), zero, zero)
    direction = res
    norm_now = inner(res, res)
    for turn in range(3):
        curved = apply_whole(direction)
        step = norm_now / inner(direction, curved)
        answer = tuple(a + step * d for a, d in zip(answer, direction))
        if turn < 2:
            res = tuple(r - step * c for r, c in zip(res, curved))
            norm_next = inner(res, res)
            ratio = norm_next / norm_now
            direction = tuple(r + ratio * d for r, d in zip(res, direction))
            norm_now = norm_next
    chosen = lax.broadcasted_iota(jnp.int32, n0.shape, 0) == me[0]
    mix = [jnp.sum(jnp.where(chosen, a, 0.0), axis=0, keepdims=True) for a in answer]
    out[...] = mix[0] * res0[:UNITS] + mix[1] * res1[:UNITS] + mix[2] * res2[:UNITS]


def body(train_ids, query_ids, embed, norm_gain, w_gate, w_up, cotangent):
    core = lax.axis_index("shard") % 2
    wide = embed.shape[1]
    w_gate_other, w_up_other = swap_core(w_gate), swap_core(w_up)

    with jax.named_scope("rows"):
        mine, other = lookup(train_ids, query_ids, embed, core)
        rows = (mine + swap_core(other)).reshape(8, 24, wide)
        rows = exchange_chips(rows)
    with jax.named_scope("normed"):
        normed = local_call(norm_kernel, shape((8, 24, wide), bf16), rows, norm_gain.reshape(1, wide))
        normed = exchange_chips(normed).reshape(192, wide)
    with jax.named_scope("acts"):
        package = local_call(
            acts_kernel, shape((PACK, 128), bf16), normed, w_gate, w_up, w_gate_other, w_up_other
        )
    with jax.named_scope("groups"):
        pair, pairs, singles = gather_groups(package)
    with jax.named_scope("cotangent"):
        cotangent, _ = lax.optimization_barrier((cotangent, pair))
        mine = lax.dynamic_slice_in_dim(cotangent, core * 64, 64, axis=0)
        columns = lax.all_to_all(
            mine.reshape(64, 16, 128).transpose(1, 0, 2), "dp", 0, 0, tiled=True
        )
        columns = jnp.take(columns, group_order(), axis=0)
        empty = jnp.zeros_like(columns)
        columns = jnp.concatenate(
            [
                jnp.concatenate([columns, empty], axis=2),
                jnp.concatenate([empty, columns], axis=2),
            ],
            axis=1,
        )

    vector = shape((BOTH, 128), f32)
    longer = shape((BOTH + 8, 128), f32)
    small = shape((8, 128), f32)
    spread = shape((8, 128, 256), bf16)
    block = shape((128, 256), bf16)
    message = shape((8, 144, 256), bf16)
    table = shape((16, 8, 128), f32)

    with jax.named_scope("rhs"):
        part, flip, acts = local_call(
            functools.partial(rhs_kernel, 1.0 / math.sqrt(2048)),
            (vector, vector, shape((BOTH, HALF), bf16)),
            *pairs,
            *singles,
            columns,
        )
        got = swap_core(flip)
    with jax.named_scope("first"):
        res0, sums, tangent = local_call(first_kernel, (vector, small, spread), part, got, acts)
        parts = exchange_chips(tangent)
        block0, shared = local_call(share_kernel, (block, message), parts, sums)
        shared = exchange_chips(shared)
        tangent0, part, flip, sums = local_call(
            curve_kernel, (spread, vector, longer, small), shared, acts
        )
        got = swap_core(flip)
    with jax.named_scope("second"):
        res1, state, tangent = local_call(
            second_kernel, (vector, small, spread), part, got, sums, res0, acts
        )
        parts = exchange_chips(tangent)
        block1, shared = local_call(share_kernel, (block, message), parts, state, block0)
        shared = exchange_chips(shared)
        past = state
        part, flip, sums = local_call(
            curve_kernel, (vector, longer, small), shared, acts, tangent0, state
        )
        got = swap_core(flip)
    with jax.named_scope("third"):
        res2, state, tangent = local_call(
            third_kernel, (vector, small, spread), part, got, sums, past, res1, res0, acts
        )
        parts = exchange_chips(tangent)
        partials = local_call(partial_kernel, table, parts, state, block0, block1)
        partials = lax.all_to_all(partials, "shard", 0, 0, tiled=True)
    with jax.named_scope("whole"):
        mine = local_call(group_kernel, table, partials, state)
        every = lax.all_to_all(mine, "dp", 0, 0, tiled=True)
        return local_call(
            whole_kernel,
            shape((UNITS, 128), f32),
            lax.axis_index("dp").reshape(1),
            every,
            res0,
            res1,
            res2,
            specs=[SMEM] + [VMEM] * 4,
        )


def solution(mesh):
    placed = (
        P("dp"),
        P("dp"),
        P("shard", None),
        P(),
        P(None, "shard"),
        P(None, "shard"),
        P("dp", None),
    )
    return jax.shard_map(
        body, mesh=mesh, in_specs=placed, out_specs=P("shard", "dp"), check_vma=False
    )
```

```python
import functools
import math

import jax
import jax.numpy as jnp
from jax import lax
from jax.experimental import pallas as pl
from jax.experimental.pallas import tpu as pltpu
from jax.sharding import PartitionSpec as P

norm_eps = 1e-05
damping = 0.1

bf16 = jnp.bfloat16
f32 = jnp.float32

STEPS = (0, -1, 1, -2, 2, -3, 3, 4)
CHIPS = [[c + 2 * i for i in range(8)] for c in range(2)]
CORE = [(i, i ^ 1) for i in range(16)]
YLO = [(i, i ^ 8) for i in range(16)]
VMEM = pl.BlockSpec(memory_space=pltpu.VMEM)
SMEM = pl.BlockSpec(memory_space=pltpu.SMEM)
UNITS = 344
BOTH = 2 * UNITS
PACK = 1040
TOKENS = 4096


def z_shift(step):
    return [(i, (i & 8) | ((i + step) & 7)) for i in range(16)]


def swap_core(v):
    return lax.ppermute(v, "shard", CORE)


def exchange_chips(v):
    return lax.all_to_all(v, "shard", 0, 0, axis_index_groups=CHIPS, tiled=True)


def local_call(kernel, outs, *args, specs=None, **more):
    return pl.pallas_call(
        kernel,
        out_shape=outs,
        in_specs=specs or [VMEM] * len(args),
        out_specs=jax.tree.map(lambda _: VMEM, outs),
        compiler_params=pltpu.CompilerParams(vmem_limit_bytes=24 * 2**20),
        **more,
    )(*args)


def shape(dims, dtype):
    return jax.ShapeDtypeStruct(dims, dtype)


def guarded(top, bottom):
    fine = bottom > 0
    return jnp.where(fine, top / jnp.where(fine, bottom, 1.0), 0.0)


def dot(a, b):
    return jnp.dot(a, b, preferred_element_type=f32)


def total(v):
    return jnp.sum(v, axis=(0, 1), keepdims=True)


def lanes(values, dims):
    lane = lax.broadcasted_iota(jnp.int32, dims, 1)
    row = lax.broadcasted_iota(jnp.int32, dims, 0)
    out = jnp.zeros(dims, f32)
    for i, v in enumerate(values):
        out = jnp.where((lane == i) & (row == 0), v, out)
    return out


def lookup_kernel(place, train, query, table, mine, other, hot):
    height = table.shape[0]

    @pl.when(pl.program_id(0) == 0)
    def _():
        core, shard = place[0], place[1]

        def column(row):
            return jnp.broadcast_to(row, (128, 128)).T

        own_train = column(train[pl.ds(core, 1), :])
        other_train = column(train[pl.ds(1 - core, 1), :])
        asked = column(query[...])
        first = core == 0
        own_query = jnp.where(first, asked[:64], asked[64:])
        other_query = jnp.where(first, asked[64:], asked[:64])
        ids = jnp.concatenate([own_train, own_query, other_train, other_query], axis=0)
        ids = ids - shard * height
        lane = lax.broadcasted_iota(jnp.int32, ids.shape, 1)
        for start in range(0, height, 128):
            wide = min(128, height - start)
            hit = jnp.where(ids == lane + start, 1.0, 0.0).astype(bf16)
            hot[:, start : start + wide] = hit[:, :wide]

    found = dot(hot[...], table[...]).astype(bf16)
    mine[...] = found[:192]
    other[...] = found[192:]


def lookup(train_ids, query_ids, embed, core):
    height, wide = embed.shape
    step = 256
    place = jnp.stack([core, lax.axis_index("shard")])
    out = shape((192, wide), bf16)
    return pl.pallas_call(
        lookup_kernel,
        grid=(wide // step,),
        out_shape=(out, out),
        in_specs=[SMEM, VMEM, VMEM, pl.BlockSpec((height, step), lambda j: (0, j))],
        out_specs=[pl.BlockSpec((192, step), lambda j: (0, j))] * 2,
        scratch_shapes=[pltpu.VMEM((384, height), bf16)],
        compiler_params=pltpu.CompilerParams(vmem_limit_bytes=24 * 2**20),
    )(place, train_ids.reshape(2, 128), query_ids.reshape(1, 128), embed)


def norm_kernel(parts, gain, out):
    rows = jnp.sum(parts[...].astype(f32), axis=0)
    inv_scale = lax.rsqrt(jnp.mean(rows * rows, axis=-1, keepdims=True) + norm_eps)
    normed = (rows * inv_scale * gain[...]).astype(bf16)
    for i in range(8):
        out[i] = normed


def acts_kernel(normed, w_gate, w_up, w_gate_other, w_up_other, out):
    rows = normed[...]

    def product(w):
        return lax.dot_general(
            w[...], rows, (((1,), (1,)), ((), ())), preferred_element_type=f32
        )

    def hidden(gate_w, up_w):
        gate = product(gate_w)
        return (gate / (1.0 + jnp.exp(-gate))) * product(up_w)

    own = hidden(w_gate, w_up)
    other = hidden(w_gate_other, w_up_other)
    asked = jnp.concatenate([own[:, 128:], other[:, 128:]], axis=1)
    fill = jnp.zeros((PACK - 3 * UNITS, 128), f32)
    out[...] = jnp.concatenate([own[:, :128], other[:, :128], asked, fill], axis=0).astype(bf16)


def gather_groups(own):
    def up(v):
        return lax.ppermute(v, "dp", z_shift(1))

    def down(v):
        return lax.ppermute(v, "dp", z_shift(-1))

    def across(v):
        return lax.ppermute(v, "dp", YLO)

    same, twin = {0: own}, {0: across(own)}
    same[-1], same[1] = up(own), down(own)
    twin[1], twin[-1] = across(same[1]), up(twin[0])
    same[-2], same[2] = up(same[-1]), down(same[1])
    twin[2], twin[-2] = across(same[2]), up(twin[-1])
    same[-3], same[3] = up(same[-2]), down(same[2])
    twin[3] = across(same[3])
    same[4] = down(same[3])
    twin[-3] = across(same[-3])
    twin[4] = down(twin[3])
    return [group[step] for step in STEPS for group in (same, twin)]


def group_order():
    me = lax.axis_index("dp")
    y, z = me // 8, me % 8
    order = []
    for step in STEPS:
        for flip in range(2):
            order.append((y ^ flip) * 8 + (z + step) % 8)
    return jnp.stack(order)


def rhs_kernel(scale, *refs):
    blocks, (wide, part, flip) = refs[:16], refs[16:]
    out = jnp.zeros((PACK - BOTH, 256), f32)
    for b in range(16):
        out = out + dot(blocks[b][BOTH:, :], wide[b])
    out = out * scale
    part[:UNITS] = out[:UNITS, :128]
    part[UNITS:] = out[:UNITS, 128:]
    flip[:UNITS] = out[:UNITS, 128:]
    flip[UNITS:] = out[:UNITS, :128]


def spread_tangent(res, blocks, tangent):
    res_t = res.T.astype(bf16)
    for i in range(8):
        acts = jnp.concatenate([blocks[2 * i][:BOTH, :], blocks[2 * i + 1][:BOTH, :]], axis=1)
        tangent[i] = dot(res_t, acts).astype(bf16)


def first_kernel(*refs):
    blocks, (part, got, res_out, sums, tangent) = refs[:16], refs[16:]
    res = part[...] + got[...]
    res_out[...] = res
    sums[...] = lanes([total(res * res)], (8, 128))
    spread_tangent(res, blocks, tangent)


def share_kernel(parts, sums, *refs):
    earlier, (block_out, message) = refs[:-2], refs[-2:]
    block = jnp.sum(parts[...].astype(f32), axis=0).astype(bf16)
    block_out[...] = block
    block = block.astype(f32)
    values = [sums[0:1, 0:1], total(block * block)]
    if earlier:
        values.append(total(block * earlier[0][...].astype(f32)))
    extra = lanes(values, (16, 256))
    hi = extra.astype(bf16).astype(f32)
    mid = (extra - hi).astype(bf16).astype(f32)
    low = extra - hi - mid
    row = lax.broadcasted_iota(jnp.int32, (16, 256), 0)
    first_row = jnp.where(row == 0, hi, 0.0)
    mid = jnp.broadcast_to(mid[0:1], (16, 256))
    low = jnp.broadcast_to(low[0:1], (16, 256))
    extra = jnp.where(row == 1, mid, jnp.where(row == 2, low, first_row))
    whole = jnp.concatenate([block, extra], axis=0).astype(bf16)
    for i in range(8):
        message[i] = whole


def curve_kernel(*refs):
    blocks, got, refs = refs[:16], refs[16], refs[17:]
    if len(refs) == 4:
        tangent_out, part, flip, sums_out = refs
    else:
        past, state, part, flip, sums_out = refs
    extra = got[0, 128:144, :].astype(f32)
    for i in range(1, 8):
        extra = extra + got[i, 128:144, :].astype(f32)
    sums = jnp.sum(extra, axis=0, keepdims=True)[:, :128]
    if len(refs) == 5:
        beta = guarded(sums[:, 0:1], state[0:1, 1:2])
    out = jnp.zeros((BOTH, 128), f32)
    for i in range(8):
        tangent = got[i, :128, :]
        if len(refs) == 4:
            tangent_out[i] = tangent
        else:
            tangent = (tangent.astype(f32) + beta * past[i].astype(f32)).astype(bf16)
        acts = jnp.concatenate([blocks[2 * i][:BOTH, :], blocks[2 * i + 1][:BOTH, :]], axis=1)
        out = out + lax.dot_general(
            acts, tangent, (((1,), (1,)), ((), ())), preferred_element_type=f32
        )
    row = lax.broadcasted_iota(jnp.int32, (8, 128), 0)
    sums = jnp.where(row == 0, jnp.broadcast_to(sums, (8, 128)), 0.0)
    sums_out[...] = sums
    part[...] = out
    flip[:UNITS] = out[UNITS:]
    flip[UNITS:BOTH] = out[:UNITS]
    flip[BOTH:] = sums


def second_kernel(*refs):
    blocks, (part, got, sums, res, res_out, state, tangent) = refs[:16], refs[16:]
    rr = sums[0:1, 0:1]
    tt = sums[0:1, 1:2] + got[BOTH : BOTH + 1, 1:2]
    inv_alpha = guarded(tt / TOKENS + damping * rr, rr)
    alpha = guarded(jnp.ones_like(inv_alpha), inv_alpha)
    old = res[...]
    new = old - alpha * ((part[...] + got[:BOTH]) / TOKENS + damping * old)
    res_out[...] = new
    state[...] = lanes([total(new * new), rr, tt, rr, inv_alpha], (8, 128))
    spread_tangent(new, blocks, tangent)


def third_kernel(*refs):
    blocks, refs = refs[:16], refs[16:]
    part, got, sums, past, res, res_before, res_out, state, tangent = refs
    rr = sums[0:1, 0:1]
    ww = sums[0:1, 1:2] + got[BOTH : BOTH + 1, 1:2]
    cross = sums[0:1, 2:3] + got[BOTH : BOTH + 1, 2:3]
    rr0, tt0, pp0, inv_alpha0 = (past[0:1, i : i + 1] for i in range(1, 5))
    beta = guarded(rr, rr0)
    tt = ww + 2.0 * beta * cross + beta * beta * tt0
    pp = rr + beta * beta * pp0
    inv_alpha = guarded(tt / TOKENS + damping * pp, rr)
    alpha = guarded(jnp.ones_like(inv_alpha), inv_alpha)
    old = res[...]
    direction = old + beta * res_before[...]
    new = old - alpha * ((part[...] + got[:BOTH]) / TOKENS + damping * direction)
    res_out[...] = new
    state[...] = lanes(
        [total(new * new), rr0, rr, tt, pp, inv_alpha0, inv_alpha, beta], (8, 128)
    )
    spread_tangent(new, blocks, tangent)


def partial_kernel(parts, state, block0, block1, message):
    block2 = jnp.sum(parts[...].astype(f32), axis=0)
    beta = state[0:1, 7:8]
    step1 = block1[...].astype(f32) + beta * block0[...].astype(f32)
    out = lanes([0.5 * state[0:1, 0:1], total(block2 * block2), total(block2 * step1)], (8, 128))
    for i in range(16):
        message[i] = out


def group_kernel(got, state, message):
    sums = jnp.sum(jnp.sum(got[...], axis=0), axis=0, keepdims=True)
    rr0, rr1, tt1, pp1, inv_alpha0, inv_alpha1, beta0 = (state[0:1, i : i + 1] for i in range(1, 8))
    rr2 = sums[:, 0:1]
    beta1 = guarded(rr2, rr1)
    tt2 = sums[:, 1:2] + 2.0 * beta1 * sums[:, 2:3] + beta1 * beta1 * tt1
    pp2 = rr2 + beta1 * beta1 * pp1
    inv_alpha2 = guarded(tt2 / TOKENS + damping * pp2, rr2)
    out = lanes([rr0, rr1, rr2, inv_alpha0, inv_alpha1, inv_alpha2, beta0, beta1], (8, 128))
    for i in range(16):
        message[i] = out


def whole_kernel(me, got, res0, res1, res2, out):
    every = jnp.sum(got[...], axis=1)
    n0, n1, n2, ia0, ia1, ia2, b0, b1 = (every[:, i : i + 1] for i in range(8))

    def apply_whole(u):
        u0, u1, u2 = u
        s0, s1, s2 = u0 - b0 * u1, u1 - b1 * u2, u2
        return s0 * ia0, s1 * ia1 - s0 * ia0, s2 * ia2 - s1 * ia1

    def inner(u, v):
        terms = u[0] * v[0] * n0 + u[1] * v[1] * n1 + u[2] * v[2] * n2
        return jnp.sum(terms, axis=0, keepdims=True)

    zero = jnp.zeros_like(n0)
    answer = (zero, zero, zero)
    res = (jnp.ones_like(n0), zero, zero)
    direction = res
    norm_now = inner(res, res)
    for turn in range(3):
        curved = apply_whole(direction)
        step = norm_now / inner(direction, curved)
        answer = tuple(a + step * d for a, d in zip(answer, direction))
        if turn < 2:
            res = tuple(r - step * c for r, c in zip(res, curved))
            norm_next = inner(res, res)
            ratio = norm_next / norm_now
            direction = tuple(r + ratio * d for r, d in zip(res, direction))
            norm_now = norm_next
    chosen = lax.broadcasted_iota(jnp.int32, n0.shape, 0) == me[0]
    mix = [jnp.sum(jnp.where(chosen, a, 0.0), axis=0, keepdims=True) for a in answer]
    out[...] = mix[0] * res0[:UNITS] + mix[1] * res1[:UNITS] + mix[2] * res2[:UNITS]


def body(train_ids, query_ids, embed, norm_gain, w_gate, w_up, cotangent):
    core = lax.axis_index("shard") % 2
    wide = embed.shape[1]
    w_gate, w_up = w_gate.T, w_up.T
    w_gate_other, w_up_other = swap_core(w_gate), swap_core(w_up)

    with jax.named_scope("rows"):
        mine, other = lookup(train_ids, query_ids, embed, core)
        rows = (mine + swap_core(other)).reshape(8, 24, wide)
        rows = exchange_chips(rows)
    with jax.named_scope("normed"):
        normed = local_call(norm_kernel, shape((8, 24, wide), bf16), rows, norm_gain.reshape(1, wide))
        normed = exchange_chips(normed).reshape(192, wide)
    with jax.named_scope("acts"):
        package = local_call(
            acts_kernel, shape((PACK, 128), bf16), normed, w_gate, w_up, w_gate_other, w_up_other
        )
    with jax.named_scope("groups"):
        blocks = gather_groups(package)
    with jax.named_scope("cotangent"):
        cotangent, _ = lax.optimization_barrier((cotangent, package))
        mine = lax.dynamic_slice_in_dim(cotangent, core * 64, 64, axis=0)
        columns = lax.all_to_all(
            mine.reshape(64, 16, 128).transpose(1, 0, 2), "dp", 0, 0, tiled=True
        )
        columns = jnp.take(columns, group_order(), axis=0)
        empty = jnp.zeros_like(columns)
        columns = jnp.concatenate(
            [
                jnp.concatenate([columns, empty], axis=2),
                jnp.concatenate([empty, columns], axis=2),
            ],
            axis=1,
        )

    vector = shape((BOTH, 128), f32)
    longer = shape((BOTH + 8, 128), f32)
    small = shape((8, 128), f32)
    spread = shape((8, 128, 256), bf16)
    block = shape((128, 256), bf16)
    message = shape((8, 144, 256), bf16)
    table = shape((16, 8, 128), f32)

    with jax.named_scope("rhs"):
        part, flip = local_call(
            functools.partial(rhs_kernel, 1.0 / math.sqrt(2048)),
            (vector, vector),
            *blocks,
            columns,
        )
        got = swap_core(flip)
    with jax.named_scope("first"):
        res0, sums, tangent = local_call(first_kernel, (vector, small, spread), *blocks, part, got)
        parts = exchange_chips(tangent)
        block0, shared = local_call(share_kernel, (block, message), parts, sums)
        shared = exchange_chips(shared)
        tangent0, part, flip, sums = local_call(
            curve_kernel, (spread, vector, longer, small), *blocks, shared
        )
        got = swap_core(flip)
    with jax.named_scope("second"):
        res1, state, tangent = local_call(
            second_kernel, (vector, small, spread), *blocks, part, got, sums, res0
        )
        parts = exchange_chips(tangent)
        block1, shared = local_call(share_kernel, (block, message), parts, state, block0)
        shared = exchange_chips(shared)
        past = state
        part, flip, sums = local_call(
            curve_kernel, (vector, longer, small), *blocks, shared, tangent0, state
        )
        got = swap_core(flip)
    with jax.named_scope("third"):
        res2, state, tangent = local_call(
            third_kernel,
            (vector, small, spread),
            *blocks,
            part,
            got,
            sums,
            past,
            res1,
            res0,
        )
        parts = exchange_chips(tangent)
        partials = local_call(partial_kernel, table, parts, state, block0, block1)
        partials = lax.all_to_all(partials, "shard", 0, 0, tiled=True)
    with jax.named_scope("whole"):
        mine = local_call(group_kernel, table, partials, state)
        every = lax.all_to_all(mine, "dp", 0, 0, tiled=True)
        return local_call(
            whole_kernel,
            shape((UNITS, 128), f32),
            lax.axis_index("dp").reshape(1),
            every,
            res0,
            res1,
            res2,
            specs=[SMEM] + [VMEM] * 4,
        )


def solution(mesh):
    placed = (
        P("dp"),
        P("dp"),
        P("shard", None),
        P(),
        P(None, "shard"),
        P(None, "shard"),
        P("dp", None),
    )
    return jax.shard_map(
        body, mesh=mesh, in_specs=placed, out_specs=P("shard", "dp"), check_vma=False
    )
```

```python
import functools
import math

import jax
import jax.numpy as jnp
from jax import lax
from jax.experimental import pallas as pl
from jax.experimental.pallas import tpu as pltpu
from jax.sharding import PartitionSpec as P

norm_eps = 1e-05
damping = 0.1

bf16 = jnp.bfloat16
f32 = jnp.float32

STEPS = (0, -1, 1, -2, 2, -3, 3, 4)
CHIPS = [[c + 2 * i for i in range(8)] for c in range(2)]
CORE = [(i, i ^ 1) for i in range(16)]
YLO = [(i, i ^ 8) for i in range(16)]
VMEM = pl.BlockSpec(memory_space=pltpu.VMEM)
SMEM = pl.BlockSpec(memory_space=pltpu.SMEM)
HBM = pl.BlockSpec(memory_space=pltpu.HBM)
UNITS = 344
BOTH = 2 * UNITS
PACK = 1040
TOKENS = 4096


def z_shift(step):
    return [(i, (i & 8) | ((i + step) & 7)) for i in range(16)]


def swap_core(v):
    return lax.ppermute(v, "shard", CORE)


def exchange_chips(v):
    return lax.all_to_all(v, "shard", 0, 0, axis_index_groups=CHIPS, tiled=True)


def local_call(kernel, outs, *args, specs=None, **more):
    return pl.pallas_call(
        kernel,
        out_shape=outs,
        in_specs=specs or [VMEM] * len(args),
        out_specs=jax.tree.map(lambda _: VMEM, outs),
        compiler_params=pltpu.CompilerParams(vmem_limit_bytes=24 * 2**20),
        **more,
    )(*args)


def shape(dims, dtype):
    return jax.ShapeDtypeStruct(dims, dtype)


def guarded(top, bottom):
    fine = bottom > 0
    return jnp.where(fine, top / jnp.where(fine, bottom, 1.0), 0.0)


def dot(a, b):
    return jnp.dot(a, b, preferred_element_type=f32)


def total(v):
    return jnp.sum(v, axis=(0, 1), keepdims=True)


def lanes(values, dims):
    lane = lax.broadcasted_iota(jnp.int32, dims, 1)
    row = lax.broadcasted_iota(jnp.int32, dims, 0)
    out = jnp.zeros(dims, f32)
    for i, v in enumerate(values):
        out = jnp.where((lane == i) & (row == 0), v, out)
    return out


LOOKUP_STEPS = 4


def lookup_kernel(place, train_hbm, query_hbm, table_hbm, mine, other, train, query, table, hot, sems):
    height, wide = table.shape
    step = wide // LOOKUP_STEPS
    asks = [
        pltpu.make_async_copy(train_hbm, train, sems.at[0]),
        pltpu.make_async_copy(query_hbm, query, sems.at[1]),
    ]
    pieces = []
    for j in range(LOOKUP_STEPS):
        span = pl.ds(j * step, step)
        pieces.append(
            pltpu.make_async_copy(table_hbm.at[:, span], table.at[:, span], sems.at[2 + j])
        )
    for copy in asks + pieces:
        copy.start()
    for copy in asks:
        copy.wait()
    shard = place[0]
    core = lax.bitwise_and(shard, 1)

    def column(row):
        return jnp.broadcast_to(row, (128, 128)).T

    own_train = column(train[pl.ds(core, 1), :])
    other_train = column(train[pl.ds(1 - core, 1), :])
    asked = column(query[...])
    first = core == 0
    own_query = jnp.where(first, asked[:64], asked[64:])
    other_query = jnp.where(first, asked[64:], asked[:64])
    ids = jnp.concatenate([own_train, own_query, other_train, other_query], axis=0)
    ids = ids - shard * height
    lane = lax.broadcasted_iota(jnp.int32, ids.shape, 1)
    for start in range(0, height, 128):
        width = min(128, height - start)
        hit = jnp.where(ids == lane + start, 1.0, 0.0).astype(bf16)
        hot[:, start : start + width] = hit[:, :width]
    for j in range(LOOKUP_STEPS):
        pieces[j].wait()
        found = dot(hot[...], table[:, j * step : (j + 1) * step]).astype(bf16)
        mine[:, j * step : (j + 1) * step] = found[:192]
        other[:, j * step : (j + 1) * step] = found[192:]


def lookup(train_ids, query_ids, embed):
    height, wide = embed.shape
    out = shape((192, wide), bf16)
    return local_call(
        lookup_kernel,
        (out, out),
        lax.axis_index("shard").reshape(1),
        train_ids.reshape(2, 128),
        query_ids.reshape(1, 128),
        embed,
        specs=[SMEM, HBM, HBM, HBM],
        scratch_shapes=[
            pltpu.VMEM((2, 128), jnp.int32),
            pltpu.VMEM((1, 128), jnp.int32),
            pltpu.VMEM((height, wide), bf16),
            pltpu.VMEM((384, height), bf16),
            pltpu.SemaphoreType.DMA((2 + LOOKUP_STEPS,)),
        ],
    )


def norm_kernel(parts, gain, out):
    rows = jnp.sum(parts[...].astype(f32), axis=0)
    inv_scale = lax.rsqrt(jnp.mean(rows * rows, axis=-1, keepdims=True) + norm_eps)
    normed = (rows * inv_scale * gain[...]).astype(bf16)
    for i in range(8):
        out[i] = normed


def acts_kernel(normed, *refs):
    weights, (out, held, sems) = refs[:4], refs[4:]
    copies = [pltpu.make_async_copy(weights[i], held.at[i], sems.at[i]) for i in range(4)]
    for copy in copies:
        copy.start()
    rows = normed[...]

    def product(i):
        copies[i].wait()
        return lax.dot_general(
            held[i], rows, (((1,), (1,)), ((), ())), preferred_element_type=f32
        )

    def hidden(i):
        gate = product(i)
        return (gate / (1.0 + jnp.exp(-gate))) * product(i + 1)

    own = hidden(0)
    other = hidden(2)
    asked = jnp.concatenate([own[:, 128:], other[:, 128:]], axis=1)
    fill = jnp.zeros((PACK - 3 * UNITS, 128), f32)
    out[...] = jnp.concatenate([own[:, :128], other[:, :128], asked, fill], axis=0).astype(bf16)


def gather_groups(own):
    def up(v):
        return lax.ppermute(v, "dp", z_shift(1))

    def down(v):
        return lax.ppermute(v, "dp", z_shift(-1))

    def across(v):
        return lax.ppermute(v, "dp", YLO)

    def together(*values):
        return lax.optimization_barrier(values)

    same, twin = {0: own}, {}
    twin[0], same[-1], same[1] = together(across(own), up(own), down(own))
    twin[1], same[-2], same[2] = together(across(same[1]), up(same[-1]), down(same[1]))
    twin[2], twin[-1], same[-3], same[3] = together(
        across(same[2]), up(twin[0]), up(same[-2]), down(same[2])
    )
    twin[3], twin[-2], same[4] = together(across(same[3]), up(twin[-1]), down(same[3]))
    twin[-3], twin[4] = across(same[-3]), down(twin[3])
    return [group[step] for step in STEPS for group in (same, twin)]


def rhs_kernel(scale, *refs):
    blocks, (me, columns, part, flip) = refs[:16], refs[16:]
    y = lax.shift_right_logical(me[0], 3)
    z = lax.bitwise_and(me[0], 7)
    empty = jnp.zeros((64, 128), bf16)
    out = jnp.zeros((PACK - BOTH, 256), f32)
    for b in range(16):
        side = y if b % 2 == 0 else 1 - y
        group = side * 8 + lax.bitwise_and(z + STEPS[b // 2], 7)
        seen = columns[group]
        wide = jnp.concatenate(
            [
                jnp.concatenate([seen, empty], axis=1),
                jnp.concatenate([empty, seen], axis=1),
            ],
            axis=0,
        )
        out = out + dot(blocks[b][BOTH:, :], wide)
    out = out * scale
    part[:UNITS] = out[:UNITS, :128]
    part[UNITS:] = out[:UNITS, 128:]
    flip[:UNITS] = out[:UNITS, 128:]
    flip[UNITS:] = out[:UNITS, :128]


def spread_tangent(res, blocks, tangent):
    res_t = res.T.astype(bf16)
    for i in range(8):
        acts = jnp.concatenate([blocks[2 * i][:BOTH, :], blocks[2 * i + 1][:BOTH, :]], axis=1)
        tangent[i] = dot(res_t, acts).astype(bf16)


def first_kernel(*refs):
    blocks, (part, got, res_out, sums, tangent) = refs[:16], refs[16:]
    res = part[...] + got[...]
    res_out[...] = res
    sums[...] = lanes([total(res * res)], (8, 128))
    spread_tangent(res, blocks, tangent)


def share_kernel(parts, sums, *refs):
    earlier, (block_out, message) = refs[:-2], refs[-2:]
    block = jnp.sum(parts[...].astype(f32), axis=0).astype(bf16)
    block_out[...] = block
    block = block.astype(f32)
    values = [sums[0:1, 0:1], total(block * block)]
    if earlier:
        values.append(total(block * earlier[0][...].astype(f32)))
    extra = lanes(values, (16, 256))
    hi = extra.astype(bf16).astype(f32)
    mid = (extra - hi).astype(bf16).astype(f32)
    low = extra - hi - mid
    row = lax.broadcasted_iota(jnp.int32, (16, 256), 0)
    first_row = jnp.where(row == 0, hi, 0.0)
    mid = jnp.broadcast_to(mid[0:1], (16, 256))
    low = jnp.broadcast_to(low[0:1], (16, 256))
    extra = jnp.where(row == 1, mid, jnp.where(row == 2, low, first_row))
    whole = jnp.concatenate([block, extra], axis=0).astype(bf16)
    for i in range(8):
        message[i] = whole


def curve_kernel(*refs):
    blocks, got, refs = refs[:16], refs[16], refs[17:]
    if len(refs) == 4:
        tangent_out, part, flip, sums_out = refs
    else:
        past, state, part, flip, sums_out = refs
    extra = got[0, 128:144, :].astype(f32)
    for i in range(1, 8):
        extra = extra + got[i, 128:144, :].astype(f32)
    sums = jnp.sum(extra, axis=0, keepdims=True)[:, :128]
    if len(refs) == 5:
        beta = guarded(sums[:, 0:1], state[0:1, 1:2])
    out = jnp.zeros((BOTH, 128), f32)
    for i in range(8):
        tangent = got[i, :128, :]
        if len(refs) == 4:
            tangent_out[i] = tangent
        else:
            tangent = (tangent.astype(f32) + beta * past[i].astype(f32)).astype(bf16)
        acts = jnp.concatenate([blocks[2 * i][:BOTH, :], blocks[2 * i + 1][:BOTH, :]], axis=1)
        out = out + lax.dot_general(
            acts, tangent, (((1,), (1,)), ((), ())), preferred_element_type=f32
        )
    row = lax.broadcasted_iota(jnp.int32, (8, 128), 0)
    sums = jnp.where(row == 0, jnp.broadcast_to(sums, (8, 128)), 0.0)
    sums_out[...] = sums
    part[...] = out
    flip[:UNITS] = out[UNITS:]
    flip[UNITS:BOTH] = out[:UNITS]
    flip[BOTH:] = sums


def second_kernel(*refs):
    blocks, (part, got, sums, res, res_out, state, tangent) = refs[:16], refs[16:]
    rr = sums[0:1, 0:1]
    tt = sums[0:1, 1:2] + got[BOTH : BOTH + 1, 1:2]
    inv_alpha = guarded(tt / TOKENS + damping * rr, rr)
    alpha = guarded(jnp.ones_like(inv_alpha), inv_alpha)
    old = res[...]
    new = old - alpha * ((part[...] + got[:BOTH]) / TOKENS + damping * old)
    res_out[...] = new
    state[...] = lanes([total(new * new), rr, tt, rr, inv_alpha], (8, 128))
    spread_tangent(new, blocks, tangent)


def third_kernel(*refs):
    blocks, refs = refs[:16], refs[16:]
    part, got, sums, past, res, res_before, res_out, state, tangent = refs
    rr = sums[0:1, 0:1]
    ww = sums[0:1, 1:2] + got[BOTH : BOTH + 1, 1:2]
    cross = sums[0:1, 2:3] + got[BOTH : BOTH + 1, 2:3]
    rr0, tt0, pp0, inv_alpha0 = (past[0:1, i : i + 1] for i in range(1, 5))
    beta = guarded(rr, rr0)
    tt = ww + 2.0 * beta * cross + beta * beta * tt0
    pp = rr + beta * beta * pp0
    inv_alpha = guarded(tt / TOKENS + damping * pp, rr)
    alpha = guarded(jnp.ones_like(inv_alpha), inv_alpha)
    old = res[...]
    direction = old + beta * res_before[...]
    new = old - alpha * ((part[...] + got[:BOTH]) / TOKENS + damping * direction)
    res_out[...] = new
    state[...] = lanes(
        [total(new * new), rr0, rr, tt, pp, inv_alpha0, inv_alpha, beta], (8, 128)
    )
    spread_tangent(new, blocks, tangent)


def partial_kernel(parts, state, block0, block1, message):
    block2 = jnp.sum(parts[...].astype(f32), axis=0)
    beta = state[0:1, 7:8]
    step1 = block1[...].astype(f32) + beta * block0[...].astype(f32)
    out = lanes([0.5 * state[0:1, 0:1], total(block2 * block2), total(block2 * step1)], (8, 128))
    for i in range(16):
        message[i] = out


def group_kernel(got, state, message):
    sums = jnp.sum(jnp.sum(got[...], axis=0), axis=0, keepdims=True)
    rr0, rr1, tt1, pp1, inv_alpha0, inv_alpha1, beta0 = (state[0:1, i : i + 1] for i in range(1, 8))
    rr2 = sums[:, 0:1]
    beta1 = guarded(rr2, rr1)
    tt2 = sums[:, 1:2] + 2.0 * beta1 * sums[:, 2:3] + beta1 * beta1 * tt1
    pp2 = rr2 + beta1 * beta1 * pp1
    inv_alpha2 = guarded(tt2 / TOKENS + damping * pp2, rr2)
    out = lanes([rr0, rr1, rr2, inv_alpha0, inv_alpha1, inv_alpha2, beta0, beta1], (8, 128))
    for i in range(16):
        message[i] = out


def whole_kernel(me, got, res0, res1, res2, out):
    every = jnp.sum(got[...], axis=1)
    n0, n1, n2, ia0, ia1, ia2, b0, b1 = (every[:, i : i + 1] for i in range(8))

    def apply_whole(u):
        u0, u1, u2 = u
        s0, s1, s2 = u0 - b0 * u1, u1 - b1 * u2, u2
        return s0 * ia0, s1 * ia1 - s0 * ia0, s2 * ia2 - s1 * ia1

    def inner(u, v):
        terms = u[0] * v[0] * n0 + u[1] * v[1] * n1 + u[2] * v[2] * n2
        return jnp.sum(terms, axis=0, keepdims=True)

    zero = jnp.zeros_like(n0)
    answer = (zero, zero, zero)
    res = (jnp.ones_like(n0), zero, zero)
    direction = res
    norm_now = inner(res, res)
    for turn in range(3):
        curved = apply_whole(direction)
        step = norm_now / inner(direction, curved)
        answer = tuple(a + step * d for a, d in zip(answer, direction))
        if turn < 2:
            res = tuple(r - step * c for r, c in zip(res, curved))
            norm_next = inner(res, res)
            ratio = norm_next / norm_now
            direction = tuple(r + ratio * d for r, d in zip(res, direction))
            norm_now = norm_next
    chosen = lax.broadcasted_iota(jnp.int32, n0.shape, 0) == me[0]
    mix = [jnp.sum(jnp.where(chosen, a, 0.0), axis=0, keepdims=True) for a in answer]
    out[...] = mix[0] * res0[:UNITS] + mix[1] * res1[:UNITS] + mix[2] * res2[:UNITS]


def body(train_ids, query_ids, embed, norm_gain, w_gate, w_up, cotangent):
    core = lax.axis_index("shard") % 2
    wide = embed.shape[1]
    w_gate, w_up = w_gate.T, w_up.T
    w_gate_other, w_up_other = swap_core(w_gate), swap_core(w_up)

    with jax.named_scope("cotangent"):
        columns = lax.dynamic_slice_in_dim(cotangent, core * 64, 64, axis=0)
        columns = lax.all_to_all(
            columns.reshape(64, 16, 128).transpose(1, 0, 2), "dp", 0, 0, tiled=True
        )
    with jax.named_scope("rows"):
        mine, other = lookup(train_ids, query_ids, embed)
        mine, other, columns = lax.optimization_barrier((mine, other, columns))
        rows = (mine + swap_core(other)).reshape(8, 24, wide)
        rows = exchange_chips(rows)
    with jax.named_scope("normed"):
        normed = local_call(norm_kernel, shape((8, 24, wide), bf16), rows, norm_gain.reshape(1, wide))
        normed = exchange_chips(normed).reshape(192, wide)
    with jax.named_scope("acts"):
        package = local_call(
            acts_kernel,
            shape((PACK, 128), bf16),
            normed,
            w_gate,
            w_up,
            w_gate_other,
            w_up_other,
            specs=[VMEM] + [HBM] * 4,
            scratch_shapes=[
                pltpu.VMEM((4, UNITS, wide), bf16),
                pltpu.SemaphoreType.DMA((4,)),
            ],
        )
    with jax.named_scope("groups"):
        blocks = gather_groups(package)
    vector = shape((BOTH, 128), f32)
    longer = shape((BOTH + 8, 128), f32)
    small = shape((8, 128), f32)
    spread = shape((8, 128, 256), bf16)
    block = shape((128, 256), bf16)
    message = shape((8, 144, 256), bf16)
    table = shape((16, 8, 128), f32)

    with jax.named_scope("rhs"):
        part, flip = local_call(
            functools.partial(rhs_kernel, 1.0 / math.sqrt(2048)),
            (vector, vector),
            *blocks,
            lax.axis_index("dp").reshape(1),
            columns,
            specs=[VMEM] * 16 + [SMEM, VMEM],
        )
        got = swap_core(flip)
    with jax.named_scope("first"):
        res0, sums, tangent = local_call(first_kernel, (vector, small, spread), *blocks, part, got)
        parts = exchange_chips(tangent)
        block0, shared = local_call(share_kernel, (block, message), parts, sums)
        shared = exchange_chips(shared)
        tangent0, part, flip, sums = local_call(
            curve_kernel, (spread, vector, longer, small), *blocks, shared
        )
        got = swap_core(flip)
    with jax.named_scope("second"):
        res1, state, tangent = local_call(
            second_kernel, (vector, small, spread), *blocks, part, got, sums, res0
        )
        parts = exchange_chips(tangent)
        block1, shared = local_call(share_kernel, (block, message), parts, state, block0)
        shared = exchange_chips(shared)
        past = state
        part, flip, sums = local_call(
            curve_kernel, (vector, longer, small), *blocks, shared, tangent0, state
        )
        got = swap_core(flip)
    with jax.named_scope("third"):
        res2, state, tangent = local_call(
            third_kernel,
            (vector, small, spread),
            *blocks,
            part,
            got,
            sums,
            past,
            res1,
            res0,
        )
        parts = exchange_chips(tangent)
        partials = local_call(partial_kernel, table, parts, state, block0, block1)
        partials = lax.all_to_all(partials, "shard", 0, 0, tiled=True)
    with jax.named_scope("whole"):
        mine = local_call(group_kernel, table, partials, state)
        every = lax.all_to_all(mine, "dp", 0, 0, tiled=True)
        return local_call(
            whole_kernel,
            shape((UNITS, 128), f32),
            lax.axis_index("dp").reshape(1),
            every,
            res0,
            res1,
            res2,
            specs=[SMEM] + [VMEM] * 4,
        )


def solution(mesh):
    placed = (
        P("dp"),
        P("dp"),
        P("shard", None),
        P(),
        P(None, "shard"),
        P(None, "shard"),
        P("dp", None),
    )
    return jax.shard_map(
        body, mesh=mesh, in_specs=placed, out_specs=P("shard", "dp"), check_vma=False
    )
```

```python
import functools
import math

import jax
import jax.numpy as jnp
from jax import lax
from jax.experimental import pallas as pl
from jax.experimental.pallas import tpu as pltpu
from jax.sharding import PartitionSpec as P

norm_eps = 1e-05
damping = 0.1

bf16 = jnp.bfloat16
f32 = jnp.float32

STEPS = (0, -1, 1, -2, 2, -3, 3, 4)
CHIPS = [[c + 2 * i for i in range(8)] for c in range(2)]
CORE = [(i, i ^ 1) for i in range(16)]
YLO = [(i, i ^ 8) for i in range(16)]
VMEM = pl.BlockSpec(memory_space=pltpu.VMEM)
SMEM = pl.BlockSpec(memory_space=pltpu.SMEM)
HBM = pl.BlockSpec(memory_space=pltpu.HBM)
UNITS = 344
BOTH = 2 * UNITS
PACK = 1040
TOKENS = 4096


def z_shift(step):
    return [(i, (i & 8) | ((i + step) & 7)) for i in range(16)]


def swap_core(v):
    return lax.ppermute(v, "shard", CORE)


def exchange_chips(v):
    return lax.all_to_all(v, "shard", 0, 0, axis_index_groups=CHIPS, tiled=True)


def local_call(kernel, outs, *args, specs=None, vmem=16, **more):
    return pl.pallas_call(
        kernel,
        out_shape=outs,
        in_specs=specs or [VMEM] * len(args),
        out_specs=jax.tree.map(lambda _: VMEM, outs),
        compiler_params=pltpu.CompilerParams(vmem_limit_bytes=vmem * 2**20),
        **more,
    )(*args)


def in_hbm(*values):
    return [pltpu.with_memory_space_constraint(v, pltpu.HBM) for v in values]


def shape(dims, dtype):
    return jax.ShapeDtypeStruct(dims, dtype)


def guarded(top, bottom):
    fine = bottom > 0
    return jnp.where(fine, top / jnp.where(fine, bottom, 1.0), 0.0)


def dot(a, b):
    return jnp.dot(a, b, preferred_element_type=f32)


def total(v):
    return jnp.sum(v, axis=(0, 1), keepdims=True)


def lanes(values, dims):
    lane = lax.broadcasted_iota(jnp.int32, dims, 1)
    row = lax.broadcasted_iota(jnp.int32, dims, 0)
    out = jnp.zeros(dims, f32)
    for i, v in enumerate(values):
        out = jnp.where((lane == i) & (row == 0), v, out)
    return out


LOOKUP_STEPS = 4


def lookup_kernel(place, train_hbm, query_hbm, table_hbm, mine, other, train, query, table, hot, sems):
    height, wide = table.shape
    step = wide // LOOKUP_STEPS
    asks = [
        pltpu.make_async_copy(train_hbm, train, sems.at[0]),
        pltpu.make_async_copy(query_hbm, query, sems.at[1]),
    ]
    pieces = []
    for j in range(LOOKUP_STEPS):
        span = pl.ds(j * step, step)
        pieces.append(
            pltpu.make_async_copy(table_hbm.at[:, span], table.at[:, span], sems.at[2 + j])
        )
    for copy in asks + pieces:
        copy.start()
    for copy in asks:
        copy.wait()
    shard = place[0]
    core = lax.bitwise_and(shard, 1)

    def column(row):
        return jnp.broadcast_to(row, (128, 128)).T

    own_train = column(train[pl.ds(core, 1), :])
    other_train = column(train[pl.ds(1 - core, 1), :])
    asked = column(query[...])
    first = core == 0
    own_query = jnp.where(first, asked[:64], asked[64:])
    other_query = jnp.where(first, asked[64:], asked[:64])
    ids = jnp.concatenate([own_train, own_query, other_train, other_query], axis=0)
    ids = ids - shard * height
    lane = lax.broadcasted_iota(jnp.int32, ids.shape, 1)
    for start in range(0, height, 128):
        width = min(128, height - start)
        hit = jnp.where(ids == lane + start, 1.0, 0.0).astype(bf16)
        hot[:, start : start + width] = hit[:, :width]
    for j in range(LOOKUP_STEPS):
        pieces[j].wait()
        found = dot(hot[...], table[:, j * step : (j + 1) * step]).astype(bf16)
        mine[:, j * step : (j + 1) * step] = found[:192]
        other[:, j * step : (j + 1) * step] = found[192:]


def lookup(train_ids, query_ids, embed):
    height, wide = embed.shape
    out = shape((192, wide), bf16)
    return local_call(
        lookup_kernel,
        (out, out),
        lax.axis_index("shard").reshape(1),
        *in_hbm(train_ids.reshape(2, 128), query_ids.reshape(1, 128), embed),
        specs=[SMEM, HBM, HBM, HBM],
        vmem=24,
        scratch_shapes=[
            pltpu.VMEM((2, 128), jnp.int32),
            pltpu.VMEM((1, 128), jnp.int32),
            pltpu.VMEM((height, wide), bf16),
            pltpu.VMEM((384, height), bf16),
            pltpu.SemaphoreType.DMA((2 + LOOKUP_STEPS,)),
        ],
    )


def add_kernel(mine, got, out):
    for i in range(8):
        out[i] = mine[i] + got[i]


def norm_kernel(parts, gain, out):
    rows = jnp.sum(parts[...].astype(f32), axis=0)
    inv_scale = lax.rsqrt(jnp.mean(rows * rows, axis=-1, keepdims=True) + norm_eps)
    normed = (rows * inv_scale * gain[...]).astype(bf16)
    for i in range(8):
        out[i] = normed


def acts_kernel(normed, w_gate, w_up, w_gate_other, w_up_other, out):
    rows = normed[...]

    def product(w):
        return lax.dot_general(
            w[...], rows, (((1,), (1,)), ((), ())), preferred_element_type=f32
        )

    def hidden(gate_w, up_w):
        gate = product(gate_w)
        return (gate / (1.0 + jnp.exp(-gate))) * product(up_w)

    own = hidden(w_gate, w_up)
    other = hidden(w_gate_other, w_up_other)
    asked = jnp.concatenate([own[:, 128:], other[:, 128:]], axis=1)
    fill = jnp.zeros((PACK - 3 * UNITS, 128), f32)
    out[...] = jnp.concatenate([own[:, :128], other[:, :128], asked, fill], axis=0).astype(bf16)


def gather_groups(own, columns):
    def up(v):
        return lax.ppermute(v, "dp", z_shift(1))

    def down(v):
        return lax.ppermute(v, "dp", z_shift(-1))

    def across(v):
        return lax.ppermute(v, "dp", YLO)

    def together(*values):
        return lax.optimization_barrier(values)

    same, twin = {0: own}, {}
    twin[0], same[-1], same[1] = across(own), up(own), down(own)
    twin[1], same[-2], same[2] = across(same[1]), up(same[-1]), down(same[1])
    same[-2], same[2], columns = together(same[-2], same[2], columns)
    twin[2], twin[-1], same[-3], same[3] = across(same[2]), up(twin[0]), up(same[-2]), down(same[2])
    twin[3], twin[-2], same[4] = across(same[3]), up(twin[-1]), down(same[3])
    twin[-3], twin[4] = across(same[-3]), down(twin[3])
    return [group[step] for step in STEPS for group in (same, twin)], columns


def rhs_kernel(scale, *refs):
    blocks, (me, columns, part, flip, acts) = refs[:16], refs[16:]
    y = lax.shift_right_logical(me[0], 3)
    z = lax.bitwise_and(me[0], 7)
    empty = jnp.zeros((64, 128), bf16)
    out = jnp.zeros((PACK - BOTH, 256), f32)
    for b in range(16):
        side = y if b % 2 == 0 else 1 - y
        group = side * 8 + lax.bitwise_and(z + STEPS[b // 2], 7)
        seen = columns[group]
        wide = jnp.concatenate(
            [
                jnp.concatenate([seen, empty], axis=1),
                jnp.concatenate([empty, seen], axis=1),
            ],
            axis=0,
        )
        out = out + dot(blocks[b][BOTH:, :], wide)
        acts[:, b * 128 : (b + 1) * 128] = blocks[b][:BOTH, :]
    out = out * scale
    part[:UNITS] = out[:UNITS, :128]
    part[UNITS:] = out[:UNITS, 128:]
    flip[:UNITS] = out[:UNITS, 128:]
    flip[UNITS:] = out[:UNITS, :128]


def spread_tangent(res, acts, tangent):
    res_t = res.T.astype(bf16)
    for i in range(8):
        tangent[i] = dot(res_t, acts[:, i * 256 : (i + 1) * 256]).astype(bf16)


def first_kernel(acts, part, got, res_out, sums, tangent):
    res = part[...] + got[...]
    res_out[...] = res
    sums[...] = lanes([total(res * res)], (8, 128))
    spread_tangent(res, acts, tangent)


def share_kernel(parts, sums, *refs):
    earlier, (block_out, message) = refs[:-2], refs[-2:]
    block = jnp.sum(parts[...].astype(f32), axis=0).astype(bf16)
    block_out[...] = block
    block = block.astype(f32)
    values = [sums[0:1, 0:1], total(block * block)]
    if earlier:
        values.append(total(block * earlier[0][...].astype(f32)))
    extra = lanes(values, (16, 256))
    hi = extra.astype(bf16).astype(f32)
    mid = (extra - hi).astype(bf16).astype(f32)
    low = extra - hi - mid
    row = lax.broadcasted_iota(jnp.int32, (16, 256), 0)
    first_row = jnp.where(row == 0, hi, 0.0)
    mid = jnp.broadcast_to(mid[0:1], (16, 256))
    low = jnp.broadcast_to(low[0:1], (16, 256))
    extra = jnp.where(row == 1, mid, jnp.where(row == 2, low, first_row))
    whole = jnp.concatenate([block, extra], axis=0).astype(bf16)
    for i in range(8):
        message[i] = whole


def curve_kernel(acts, got, *refs):
    if len(refs) == 4:
        tangent_out, part, flip, sums_out = refs
    else:
        past, state, part, flip, sums_out = refs
    extra = got[0, 128:144, :].astype(f32)
    for i in range(1, 8):
        extra = extra + got[i, 128:144, :].astype(f32)
    sums = jnp.sum(extra, axis=0, keepdims=True)[:, :128]
    if len(refs) == 5:
        beta = guarded(sums[:, 0:1], state[0:1, 1:2])
    out = jnp.zeros((BOTH, 128), f32)
    for i in range(8):
        tangent = got[i, :128, :]
        if len(refs) == 4:
            tangent_out[i] = tangent
        else:
            tangent = (tangent.astype(f32) + beta * past[i].astype(f32)).astype(bf16)
        out = out + lax.dot_general(
            acts[:, i * 256 : (i + 1) * 256],
            tangent,
            (((1,), (1,)), ((), ())),
            preferred_element_type=f32,
        )
    row = lax.broadcasted_iota(jnp.int32, (8, 128), 0)
    sums = jnp.where(row == 0, jnp.broadcast_to(sums, (8, 128)), 0.0)
    sums_out[...] = sums
    part[...] = out
    flip[:UNITS] = out[UNITS:]
    flip[UNITS:BOTH] = out[:UNITS]
    flip[BOTH:] = sums


def second_kernel(acts, part, got, sums, res, res_out, state, tangent):
    rr = sums[0:1, 0:1]
    tt = sums[0:1, 1:2] + got[BOTH : BOTH + 1, 1:2]
    inv_alpha = guarded(tt / TOKENS + damping * rr, rr)
    alpha = guarded(jnp.ones_like(inv_alpha), inv_alpha)
    old = res[...]
    new = old - alpha * ((part[...] + got[:BOTH]) / TOKENS + damping * old)
    res_out[...] = new
    state[...] = lanes([total(new * new), rr, tt, rr, inv_alpha], (8, 128))
    spread_tangent(new, acts, tangent)


def third_kernel(acts, part, got, sums, past, res, res_before, res_out, state, tangent):
    rr = sums[0:1, 0:1]
    ww = sums[0:1, 1:2] + got[BOTH : BOTH + 1, 1:2]
    cross = sums[0:1, 2:3] + got[BOTH : BOTH + 1, 2:3]
    rr0, tt0, pp0, inv_alpha0 = (past[0:1, i : i + 1] for i in range(1, 5))
    beta = guarded(rr, rr0)
    tt = ww + 2.0 * beta * cross + beta * beta * tt0
    pp = rr + beta * beta * pp0
    inv_alpha = guarded(tt / TOKENS + damping * pp, rr)
    alpha = guarded(jnp.ones_like(inv_alpha), inv_alpha)
    old = res[...]
    direction = old + beta * res_before[...]
    new = old - alpha * ((part[...] + got[:BOTH]) / TOKENS + damping * direction)
    res_out[...] = new
    state[...] = lanes(
        [total(new * new), rr0, rr, tt, pp, inv_alpha0, inv_alpha, beta], (8, 128)
    )
    spread_tangent(new, acts, tangent)


def partial_kernel(parts, state, block0, block1, message):
    block2 = jnp.sum(parts[...].astype(f32), axis=0)
    beta = state[0:1, 7:8]
    step1 = block1[...].astype(f32) + beta * block0[...].astype(f32)
    out = lanes([0.5 * state[0:1, 0:1], total(block2 * block2), total(block2 * step1)], (8, 128))
    for i in range(16):
        message[i] = out


def group_kernel(got, state, message):
    sums = jnp.sum(jnp.sum(got[...], axis=0), axis=0, keepdims=True)
    rr0, rr1, tt1, pp1, inv_alpha0, inv_alpha1, beta0 = (state[0:1, i : i + 1] for i in range(1, 8))
    rr2 = sums[:, 0:1]
    beta1 = guarded(rr2, rr1)
    tt2 = sums[:, 1:2] + 2.0 * beta1 * sums[:, 2:3] + beta1 * beta1 * tt1
    pp2 = rr2 + beta1 * beta1 * pp1
    inv_alpha2 = guarded(tt2 / TOKENS + damping * pp2, rr2)
    out = lanes([rr0, rr1, rr2, inv_alpha0, inv_alpha1, inv_alpha2, beta0, beta1], (8, 128))
    for i in range(16):
        message[i] = out


def whole_kernel(me, got, res0, res1, res2, out):
    every = jnp.sum(got[...], axis=1)
    n0, n1, n2, ia0, ia1, ia2, b0, b1 = (every[:, i : i + 1] for i in range(8))

    def apply_whole(u):
        u0, u1, u2 = u
        s0, s1, s2 = u0 - b0 * u1, u1 - b1 * u2, u2
        return s0 * ia0, s1 * ia1 - s0 * ia0, s2 * ia2 - s1 * ia1

    def inner(u, v):
        terms = u[0] * v[0] * n0 + u[1] * v[1] * n1 + u[2] * v[2] * n2
        return jnp.sum(terms, axis=0, keepdims=True)

    zero = jnp.zeros_like(n0)
    answer = (zero, zero, zero)
    res = (jnp.ones_like(n0), zero, zero)
    direction = res
    norm_now = inner(res, res)
    for turn in range(3):
        curved = apply_whole(direction)
        step = norm_now / inner(direction, curved)
        answer = tuple(a + step * d for a, d in zip(answer, direction))
        if turn < 2:
            res = tuple(r - step * c for r, c in zip(res, curved))
            norm_next = inner(res, res)
            ratio = norm_next / norm_now
            direction = tuple(r + ratio * d for r, d in zip(res, direction))
            norm_now = norm_next
    chosen = lax.broadcasted_iota(jnp.int32, n0.shape, 0) == me[0]
    mix = [jnp.sum(jnp.where(chosen, a, 0.0), axis=0, keepdims=True) for a in answer]
    out[...] = mix[0] * res0[:UNITS] + mix[1] * res1[:UNITS] + mix[2] * res2[:UNITS]


def body(train_ids, query_ids, embed, norm_gain, w_gate, w_up, cotangent):
    core = lax.axis_index("shard") % 2
    wide = embed.shape[1]
    w_gate, w_up = w_gate.T, w_up.T
    w_gate_other, w_up_other = swap_core(w_gate), swap_core(w_up)

    with jax.named_scope("rows"):
        mine, other = lookup(train_ids, query_ids, embed)
        other = swap_core(other).reshape(8, 24, wide)
        rows = local_call(
            add_kernel, pltpu.VMEM((8, 24, wide), bf16), mine.reshape(8, 24, wide), other
        )
        rows = exchange_chips(rows)
    with jax.named_scope("normed"):
        normed = local_call(
            norm_kernel, pltpu.VMEM((8, 24, wide), bf16), rows, norm_gain.reshape(1, wide)
        )
    with jax.named_scope("normed"):
        normed = exchange_chips(normed).reshape(192, wide)
    with jax.named_scope("acts"):
        package = local_call(
            acts_kernel, shape((PACK, 128), bf16), normed, w_gate, w_up, w_gate_other, w_up_other
        )
    with jax.named_scope("groups"):
        columns = lax.dynamic_slice_in_dim(cotangent, core * 64, 64, axis=0)
        columns = columns.reshape(64, 16, 128).transpose(1, 0, 2)
        columns, package = lax.optimization_barrier((columns, package))
        columns = lax.all_to_all(columns, "dp", 0, 0, tiled=True)
        blocks, columns = gather_groups(package, columns)
    vector = shape((BOTH, 128), f32)
    longer = shape((BOTH + 8, 128), f32)
    small = shape((8, 128), f32)
    spread = shape((8, 128, 256), bf16)
    block = shape((128, 256), bf16)
    message = shape((8, 144, 256), bf16)
    table = shape((16, 8, 128), f32)

    with jax.named_scope("rhs"):
        part, flip, acts = local_call(
            functools.partial(rhs_kernel, 1.0 / math.sqrt(2048)),
            (vector, vector, pltpu.VMEM((BOTH, TOKENS // 2), bf16)),
            *blocks,
            lax.axis_index("dp").reshape(1),
            columns,
            specs=[VMEM] * 16 + [SMEM, VMEM],
        )
        got = swap_core(flip)
    with jax.named_scope("first"):
        res0, sums, tangent = local_call(first_kernel, (vector, small, spread), acts, part, got)
        parts = exchange_chips(tangent)
        block0, shared = local_call(share_kernel, (block, message), parts, sums)
        shared = exchange_chips(shared)
        tangent0, part, flip, sums = local_call(
            curve_kernel, (spread, vector, longer, small), acts, shared
        )
        got = swap_core(flip)
    with jax.named_scope("second"):
        res1, state, tangent = local_call(
            second_kernel, (vector, small, spread), acts, part, got, sums, res0
        )
        parts = exchange_chips(tangent)
        block1, shared = local_call(share_kernel, (block, message), parts, state, block0)
        shared = exchange_chips(shared)
        past = state
        part, flip, sums = local_call(
            curve_kernel, (vector, longer, small), acts, shared, tangent0, state
        )
        got = swap_core(flip)
    with jax.named_scope("third"):
        res2, state, tangent = local_call(
            third_kernel,
            (vector, small, spread),
            acts,
            part,
            got,
            sums,
            past,
            res1,
            res0,
        )
        parts = exchange_chips(tangent)
        partials = local_call(partial_kernel, table, parts, state, block0, block1)
        partials = lax.all_to_all(partials, "shard", 0, 0, tiled=True)
    with jax.named_scope("whole"):
        mine = local_call(group_kernel, table, partials, state)
        every = lax.all_to_all(mine, "dp", 0, 0, tiled=True)
        return local_call(
            whole_kernel,
            shape((UNITS, 128), f32),
            lax.axis_index("dp").reshape(1),
            every,
            res0,
            res1,
            res2,
            specs=[SMEM] + [VMEM] * 4,
        )


def solution(mesh):
    placed = (
        P("dp"),
        P("dp"),
        P("shard", None),
        P(),
        P(None, "shard"),
        P(None, "shard"),
        P("dp", None),
    )
    return jax.shard_map(
        body, mesh=mesh, in_specs=placed, out_specs=P("shard", "dp"), check_vma=False
    )
```

```python
import functools
import math

import jax
import jax.numpy as jnp
from jax import lax
from jax.experimental import pallas as pl
from jax.experimental.pallas import tpu as pltpu
from jax.sharding import PartitionSpec as P

norm_eps = 1e-05
damping = 0.1

bf16 = jnp.bfloat16
f32 = jnp.float32

STEPS = (0, -1, 1, -2, 2, -3, 3, 4)
CHIPS = [[c + 2 * i for i in range(8)] for c in range(2)]
CORE = [(i, i ^ 1) for i in range(16)]
YLO = [(i, i ^ 8) for i in range(16)]
VMEM = pl.BlockSpec(memory_space=pltpu.VMEM)
SMEM = pl.BlockSpec(memory_space=pltpu.SMEM)
HBM = pl.BlockSpec(memory_space=pltpu.HBM)
UNITS = 344
BOTH = 2 * UNITS
PACK = 1040
TOKENS = 4096


def z_shift(step):
    return [(i, (i & 8) | ((i + step) & 7)) for i in range(16)]


def swap_core(v):
    return lax.ppermute(v, "shard", CORE)


def exchange_chips(v):
    return lax.all_to_all(v, "shard", 0, 0, axis_index_groups=CHIPS, tiled=True)


def local_call(kernel, outs, *args, specs=None, vmem=16, **more):
    return pl.pallas_call(
        kernel,
        out_shape=outs,
        in_specs=specs or [VMEM] * len(args),
        out_specs=jax.tree.map(lambda _: VMEM, outs),
        compiler_params=pltpu.CompilerParams(vmem_limit_bytes=vmem * 2**20),
        **more,
    )(*args)


def in_hbm(*values):
    return [pltpu.with_memory_space_constraint(v, pltpu.HBM) for v in values]


def shape(dims, dtype):
    return jax.ShapeDtypeStruct(dims, dtype)


def guarded(top, bottom):
    fine = bottom > 0
    return jnp.where(fine, top / jnp.where(fine, bottom, 1.0), 0.0)


def dot(a, b):
    return jnp.dot(a, b, preferred_element_type=f32)


def total(v):
    return jnp.sum(v, axis=(0, 1), keepdims=True)


def lanes(values, dims):
    lane = lax.broadcasted_iota(jnp.int32, dims, 1)
    row = lax.broadcasted_iota(jnp.int32, dims, 0)
    out = jnp.zeros(dims, f32)
    for i, v in enumerate(values):
        out = jnp.where((lane == i) & (row == 0), v, out)
    return out


LOOKUP_STEPS = 4


def lookup_kernel(place, train_hbm, query_hbm, table_hbm, mine, other, train, query, table, hot, sems):
    height, wide = table.shape
    step = wide // LOOKUP_STEPS
    asks = [
        pltpu.make_async_copy(train_hbm, train, sems.at[0]),
        pltpu.make_async_copy(query_hbm, query, sems.at[1]),
    ]
    pieces = []
    for j in range(LOOKUP_STEPS):
        span = pl.ds(j * step, step)
        pieces.append(
            pltpu.make_async_copy(table_hbm.at[:, span], table.at[:, span], sems.at[2 + j])
        )
    for copy in asks + pieces:
        copy.start()
    for copy in asks:
        copy.wait()
    shard = place[0]
    core = lax.bitwise_and(shard, 1)

    def column(row):
        return jnp.broadcast_to(row, (128, 128)).T

    own_train = column(train[pl.ds(core, 1), :])
    other_train = column(train[pl.ds(1 - core, 1), :])
    asked = column(query[...])
    first = core == 0
    own_query = jnp.where(first, asked[:64], asked[64:])
    other_query = jnp.where(first, asked[64:], asked[:64])
    ids = jnp.concatenate([own_train, own_query, other_train, other_query], axis=0)
    ids = ids - shard * height
    lane = lax.broadcasted_iota(jnp.int32, ids.shape, 1)
    for start in range(0, height, 128):
        width = min(128, height - start)
        hit = jnp.where(ids == lane + start, 1.0, 0.0).astype(bf16)
        hot[:, start : start + width] = hit[:, :width]
    for j in range(LOOKUP_STEPS):
        pieces[j].wait()
        found = dot(hot[...], table[:, j * step : (j + 1) * step]).astype(bf16)
        mine[:, j * step : (j + 1) * step] = found[:192]
        other[:, j * step : (j + 1) * step] = found[192:]


def lookup(train_ids, query_ids, embed):
    height, wide = embed.shape
    out = shape((192, wide), bf16)
    return local_call(
        lookup_kernel,
        (out, out),
        lax.axis_index("shard").reshape(1),
        *in_hbm(train_ids.reshape(2, 128), query_ids.reshape(1, 128), embed),
        specs=[SMEM, HBM, HBM, HBM],
        vmem=24,
        scratch_shapes=[
            pltpu.VMEM((2, 128), jnp.int32),
            pltpu.VMEM((1, 128), jnp.int32),
            pltpu.VMEM((height, wide), bf16),
            pltpu.VMEM((384, height), bf16),
            pltpu.SemaphoreType.DMA((2 + LOOKUP_STEPS,)),
        ],
    )


def add_kernel(mine, got, out):
    for i in range(8):
        out[i] = mine[i] + got[i]


def norm_kernel(parts, gain, out):
    rows = parts[0]
    for i in range(1, 8):
        rows = rows + parts[i]
    rows = rows.astype(f32)
    inv_scale = lax.rsqrt(jnp.mean(rows * rows, axis=-1, keepdims=True) + norm_eps)
    normed = (rows * inv_scale * gain[...]).astype(bf16)
    for i in range(8):
        out[i] = normed


def acts_kernel(normed, w_gate, w_up, w_gate_other, w_up_other, out):
    rows = normed[...].T

    def product(w):
        return dot(w[...], rows)

    def hidden(gate_w, up_w):
        gate = product(gate_w)
        return (gate / (1.0 + jnp.exp(-gate))) * product(up_w)

    own = hidden(w_gate, w_up)
    other = hidden(w_gate_other, w_up_other)
    asked = jnp.concatenate([own[:, 128:], other[:, 128:]], axis=1)
    fill = jnp.zeros((PACK - 3 * UNITS, 128), f32)
    out[...] = jnp.concatenate([own[:, :128], other[:, :128], asked, fill], axis=0).astype(bf16)


def gather_groups(own, columns):
    def up(v):
        return lax.ppermute(v, "dp", z_shift(1))

    def down(v):
        return lax.ppermute(v, "dp", z_shift(-1))

    def across(v):
        return lax.ppermute(v, "dp", YLO)

    def together(*values):
        return lax.optimization_barrier(values)

    same, twin = {0: own}, {}
    twin[0], same[-1], same[1] = across(own), up(own), down(own)
    twin[1], same[-2], same[2] = across(same[1]), up(same[-1]), down(same[1])
    twin[2], twin[-1], same[-3], same[3] = across(same[2]), up(twin[0]), up(same[-2]), down(same[2])
    twin[3], twin[-2], same[4] = across(same[3]), up(twin[-1]), down(same[3])
    twin[-3], twin[4] = across(same[-3]), down(twin[3])
    return [group[step] for step in STEPS for group in (same, twin)], columns


def rhs_kernel(scale, *refs):
    blocks, (me, columns, part, flip, acts) = refs[:16], refs[16:]
    y = lax.shift_right_logical(me[0], 3)
    z = lax.bitwise_and(me[0], 7)
    empty = jnp.zeros((64, 128), bf16)
    out = jnp.zeros((PACK - BOTH, 256), f32)
    for i, step in enumerate(STEPS):
        pieces = []
        for side in (y, 1 - y):
            seen = columns[side * 8 + lax.bitwise_and(z + step, 7)]
            pieces.append(jnp.concatenate([seen, empty], axis=1))
            pieces.append(jnp.concatenate([empty, seen], axis=1))
        pair = blocks[2 * i], blocks[2 * i + 1]
        asked = jnp.concatenate([block[BOTH:, :] for block in pair], axis=1)
        out = out + dot(asked, jnp.concatenate(pieces, axis=0))
        for j, block in enumerate(pair):
            acts[:, (2 * i + j) * 128 : (2 * i + j + 1) * 128] = block[:BOTH, :]
    out = out * scale
    part[:UNITS] = out[:UNITS, :128]
    part[UNITS:] = out[:UNITS, 128:]
    flip[:UNITS] = out[:UNITS, 128:]
    flip[UNITS:] = out[:UNITS, :128]


def spread_tangent(res, acts, tangent):
    res_t = res.T.astype(bf16)
    for i in range(8):
        tangent[i] = dot(res_t, acts[:, i * 256 : (i + 1) * 256]).astype(bf16)


def first_kernel(acts, part, got, res_out, sums, tangent):
    res = part[...] + got[...]
    res_out[...] = res
    sums[...] = lanes([total(res * res)], (8, 128))
    spread_tangent(res, acts, tangent)


def share_kernel(parts, sums, *refs):
    earlier, (block_out, message) = refs[:-2], refs[-2:]
    block = jnp.sum(parts[...].astype(f32), axis=0).astype(bf16)
    block_out[...] = block
    block = block.astype(f32)
    values = [sums[0:1, 0:1], total(block * block)]
    if earlier:
        values.append(total(block * earlier[0][...].astype(f32)))
    extra = lanes(values, (16, 256))
    hi = extra.astype(bf16).astype(f32)
    mid = (extra - hi).astype(bf16).astype(f32)
    low = extra - hi - mid
    row = lax.broadcasted_iota(jnp.int32, (16, 256), 0)
    first_row = jnp.where(row == 0, hi, 0.0)
    mid = jnp.broadcast_to(mid[0:1], (16, 256))
    low = jnp.broadcast_to(low[0:1], (16, 256))
    extra = jnp.where(row == 1, mid, jnp.where(row == 2, low, first_row))
    whole = jnp.concatenate([block, extra], axis=0).astype(bf16)
    for i in range(8):
        message[i] = whole


def curve_kernel(acts, got, *refs):
    if len(refs) == 4:
        tangent_out, part, flip, sums_out = refs
    else:
        past, state, part, flip, sums_out = refs
    extra = got[0, 128:144, :].astype(f32)
    for i in range(1, 8):
        extra = extra + got[i, 128:144, :].astype(f32)
    sums = jnp.sum(extra, axis=0, keepdims=True)[:, :128]
    if len(refs) == 5:
        beta = guarded(sums[:, 0:1], state[0:1, 1:2])
    out = jnp.zeros((BOTH, 128), f32)
    for i in range(8):
        tangent = got[i, :128, :]
        if len(refs) == 4:
            tangent_out[i] = tangent
        else:
            tangent = (tangent.astype(f32) + beta * past[i].astype(f32)).astype(bf16)
        out = out + lax.dot_general(
            acts[:, i * 256 : (i + 1) * 256],
            tangent,
            (((1,), (1,)), ((), ())),
            preferred_element_type=f32,
        )
    row = lax.broadcasted_iota(jnp.int32, (8, 128), 0)
    sums = jnp.where(row == 0, jnp.broadcast_to(sums, (8, 128)), 0.0)
    sums_out[...] = sums
    part[...] = out
    flip[:UNITS] = out[UNITS:]
    flip[UNITS:BOTH] = out[:UNITS]
    flip[BOTH:] = sums


def second_kernel(acts, part, got, sums, res, res_out, state, tangent):
    rr = sums[0:1, 0:1]
    tt = sums[0:1, 1:2] + got[BOTH : BOTH + 1, 1:2]
    inv_alpha = guarded(tt / TOKENS + damping * rr, rr)
    alpha = guarded(jnp.ones_like(inv_alpha), inv_alpha)
    old = res[...]
    new = old - alpha * ((part[...] + got[:BOTH]) / TOKENS + damping * old)
    res_out[...] = new
    state[...] = lanes([total(new * new), rr, tt, rr, inv_alpha], (8, 128))
    spread_tangent(new, acts, tangent)


def third_kernel(acts, part, got, sums, past, res, res_before, res_out, state, tangent):
    rr = sums[0:1, 0:1]
    ww = sums[0:1, 1:2] + got[BOTH : BOTH + 1, 1:2]
    cross = sums[0:1, 2:3] + got[BOTH : BOTH + 1, 2:3]
    rr0, tt0, pp0, inv_alpha0 = (past[0:1, i : i + 1] for i in range(1, 5))
    beta = guarded(rr, rr0)
    tt = ww + 2.0 * beta * cross + beta * beta * tt0
    pp = rr + beta * beta * pp0
    inv_alpha = guarded(tt / TOKENS + damping * pp, rr)
    alpha = guarded(jnp.ones_like(inv_alpha), inv_alpha)
    old = res[...]
    direction = old + beta * res_before[...]
    new = old - alpha * ((part[...] + got[:BOTH]) / TOKENS + damping * direction)
    res_out[...] = new
    state[...] = lanes(
        [total(new * new), rr0, rr, tt, pp, inv_alpha0, inv_alpha, beta], (8, 128)
    )
    spread_tangent(new, acts, tangent)


def partial_kernel(parts, state, block0, block1, message):
    block2 = jnp.sum(parts[...].astype(f32), axis=0)
    beta = state[0:1, 7:8]
    step1 = block1[...].astype(f32) + beta * block0[...].astype(f32)
    out = lanes([0.5 * state[0:1, 0:1], total(block2 * block2), total(block2 * step1)], (1, 128))
    for i in range(16):
        message[i] = out


def group_kernel(got, state, message):
    sums = jnp.sum(got[...], axis=0)
    rr0, rr1, tt1, pp1, inv_alpha0, inv_alpha1, beta0 = (state[0:1, i : i + 1] for i in range(1, 8))
    rr2 = sums[:, 0:1]
    beta1 = guarded(rr2, rr1)
    tt2 = sums[:, 1:2] + 2.0 * beta1 * sums[:, 2:3] + beta1 * beta1 * tt1
    pp2 = rr2 + beta1 * beta1 * pp1
    inv_alpha2 = guarded(tt2 / TOKENS + damping * pp2, rr2)
    out = lanes([rr0, rr1, rr2, inv_alpha0, inv_alpha1, inv_alpha2, beta0, beta1], (1, 128))
    for i in range(16):
        message[i] = out


def whole_kernel(me, got, res0, res1, res2, out):
    every = jnp.concatenate([got[i] for i in range(16)], axis=0)
    n0, n1, n2, ia0, ia1, ia2, b0, b1 = (every[:, i : i + 1] for i in range(8))

    def apply_whole(u):
        u0, u1, u2 = u
        s0, s1, s2 = u0 - b0 * u1, u1 - b1 * u2, u2
        return s0 * ia0, s1 * ia1 - s0 * ia0, s2 * ia2 - s1 * ia1

    def inner(u, v):
        terms = u[0] * v[0] * n0 + u[1] * v[1] * n1 + u[2] * v[2] * n2
        return jnp.sum(terms, axis=0, keepdims=True)

    zero = jnp.zeros_like(n0)
    answer = (zero, zero, zero)
    res = (jnp.ones_like(n0), zero, zero)
    direction = res
    norm_now = inner(res, res)
    for turn in range(3):
        curved = apply_whole(direction)
        step = norm_now / inner(direction, curved)
        answer = tuple(a + step * d for a, d in zip(answer, direction))
        if turn < 2:
            res = tuple(r - step * c for r, c in zip(res, curved))
            norm_next = inner(res, res)
            ratio = norm_next / norm_now
            direction = tuple(r + ratio * d for r, d in zip(res, direction))
            norm_now = norm_next
    chosen = lax.broadcasted_iota(jnp.int32, n0.shape, 0) == me[0]
    mix = [jnp.sum(jnp.where(chosen, a, 0.0), axis=0, keepdims=True) for a in answer]
    out[...] = mix[0] * res0[:UNITS] + mix[1] * res1[:UNITS] + mix[2] * res2[:UNITS]


def body(train_ids, query_ids, embed, norm_gain, w_gate, w_up, cotangent):
    core = lax.axis_index("shard") % 2
    wide = embed.shape[1]
    w_gate, w_up = w_gate.T, w_up.T
    w_gate_other, w_up_other = swap_core(w_gate), swap_core(w_up)

    with jax.named_scope("rows"):
        mine, other = lookup(train_ids, query_ids, embed)
        other = swap_core(other).reshape(8, 24, wide)
        rows = local_call(
            add_kernel, pltpu.VMEM((8, 24, wide), bf16), mine.reshape(8, 24, wide), other
        )
        rows = exchange_chips(rows)
    with jax.named_scope("normed"):
        normed = local_call(
            norm_kernel, pltpu.VMEM((8, 24, wide), bf16), rows, norm_gain.reshape(1, wide)
        )
    with jax.named_scope("normed"):
        normed = exchange_chips(normed).reshape(192, wide)
    with jax.named_scope("acts"):
        package = local_call(
            acts_kernel, shape((PACK, 128), bf16), normed, w_gate, w_up, w_gate_other, w_up_other
        )
    with jax.named_scope("groups"):
        columns = lax.dynamic_slice_in_dim(cotangent, core * 64, 64, axis=0)
        columns = columns.reshape(64, 16, 128).transpose(1, 0, 2)
        columns, package = lax.optimization_barrier((columns, package))
        columns = lax.all_to_all(columns, "dp", 0, 0, tiled=True)
        blocks, columns = gather_groups(package, columns)
    vector = shape((BOTH, 128), f32)
    longer = shape((BOTH + 8, 128), f32)
    small = shape((8, 128), f32)
    spread = shape((8, 128, 256), bf16)
    block = shape((128, 256), bf16)
    message = shape((8, 144, 256), bf16)
    table = shape((16, 1, 128), f32)

    with jax.named_scope("rhs"):
        part, flip, acts = local_call(
            functools.partial(rhs_kernel, 1.0 / math.sqrt(2048)),
            (vector, vector, pltpu.VMEM((BOTH, TOKENS // 2), bf16)),
            *blocks,
            lax.axis_index("dp").reshape(1),
            columns,
            specs=[VMEM] * 16 + [SMEM, VMEM],
        )
        got = swap_core(flip)
    with jax.named_scope("first"):
        res0, sums, tangent = local_call(first_kernel, (vector, small, spread), acts, part, got)
        parts = exchange_chips(tangent)
        block0, shared = local_call(share_kernel, (block, message), parts, sums)
        shared = exchange_chips(shared)
        tangent0, part, flip, sums = local_call(
            curve_kernel, (spread, vector, longer, small), acts, shared
        )
        got = swap_core(flip)
    with jax.named_scope("second"):
        res1, state, tangent = local_call(
            second_kernel, (vector, small, spread), acts, part, got, sums, res0
        )
        parts = exchange_chips(tangent)
        block1, shared = local_call(share_kernel, (block, message), parts, state, block0)
        shared = exchange_chips(shared)
        past = state
        part, flip, sums = local_call(
            curve_kernel, (vector, longer, small), acts, shared, tangent0, state
        )
        got = swap_core(flip)
    with jax.named_scope("third"):
        res2, state, tangent = local_call(
            third_kernel,
            (vector, small, spread),
            acts,
            part,
            got,
            sums,
            past,
            res1,
            res0,
        )
        parts = exchange_chips(tangent)
        partials = local_call(partial_kernel, table, parts, state, block0, block1)
        partials = lax.all_to_all(partials, "shard", 0, 0, tiled=True)
    with jax.named_scope("whole"):
        mine = local_call(group_kernel, table, partials, state)
        every = lax.all_to_all(mine, "dp", 0, 0, tiled=True)
        return local_call(
            whole_kernel,
            shape((UNITS, 128), f32),
            lax.axis_index("dp").reshape(1),
            every,
            res0,
            res1,
            res2,
            specs=[SMEM] + [VMEM] * 4,
        )


def solution(mesh):
    placed = (
        P("dp"),
        P("dp"),
        P("shard", None),
        P(),
        P(None, "shard"),
        P(None, "shard"),
        P("dp", None),
    )
    return jax.shard_map(
        body, mesh=mesh, in_specs=placed, out_specs=P("shard", "dp"), check_vma=False
    )
```

```python
import functools
import math

import jax
import jax.numpy as jnp
from jax import lax
from jax.experimental import pallas as pl
from jax.experimental.pallas import tpu as pltpu
from jax.sharding import PartitionSpec as P

norm_eps = 1e-05
damping = 0.1

bf16 = jnp.bfloat16
f32 = jnp.float32

STEPS = (0, -1, 1, -2, 2, -3, 3, 4)
CHIPS = [[c + 2 * i for i in range(8)] for c in range(2)]
CORE = [(i, i ^ 1) for i in range(16)]
YLO = [(i, i ^ 8) for i in range(16)]
VMEM = pl.BlockSpec(memory_space=pltpu.VMEM)
SMEM = pl.BlockSpec(memory_space=pltpu.SMEM)
HBM = pl.BlockSpec(memory_space=pltpu.HBM)
UNITS = 344
BOTH = 2 * UNITS
PACK = 1040
TOKENS = 4096


def z_shift(step):
    return [(i, (i & 8) | ((i + step) & 7)) for i in range(16)]


def swap_core(v):
    return lax.ppermute(v, "shard", CORE)


def exchange_chips(v):
    return lax.all_to_all(v, "shard", 0, 0, axis_index_groups=CHIPS, tiled=True)


def local_call(kernel, outs, *args, specs=None, vmem=16, **more):
    return pl.pallas_call(
        kernel,
        out_shape=outs,
        in_specs=specs or [VMEM] * len(args),
        out_specs=jax.tree.map(lambda _: VMEM, outs),
        compiler_params=pltpu.CompilerParams(vmem_limit_bytes=vmem * 2**20),
        **more,
    )(*args)


def in_hbm(*values):
    return [pltpu.with_memory_space_constraint(v, pltpu.HBM) for v in values]


def shape(dims, dtype):
    return jax.ShapeDtypeStruct(dims, dtype)


def guarded(top, bottom):
    fine = bottom > 0
    return jnp.where(fine, top / jnp.where(fine, bottom, 1.0), 0.0)


def dot(a, b):
    return jnp.dot(a, b, preferred_element_type=f32)


def total(v):
    return jnp.sum(v, axis=(0, 1), keepdims=True)


def lanes(values, dims):
    lane = lax.broadcasted_iota(jnp.int32, dims, 1)
    row = lax.broadcasted_iota(jnp.int32, dims, 0)
    out = jnp.zeros(dims, f32)
    for i, v in enumerate(values):
        out = jnp.where((lane == i) & (row == 0), v, out)
    return out


LOOKUP_STEPS = 4


def lookup_kernel(place, train_hbm, query_hbm, table_hbm, mine, other, train, query, table, hot, sems):
    height, wide = table.shape
    step = wide // LOOKUP_STEPS
    asks = [
        pltpu.make_async_copy(train_hbm, train, sems.at[0]),
        pltpu.make_async_copy(query_hbm, query, sems.at[1]),
    ]
    pieces = []
    for j in range(LOOKUP_STEPS):
        span = pl.ds(j * step, step)
        pieces.append(
            pltpu.make_async_copy(table_hbm.at[:, span], table.at[:, span], sems.at[2 + j])
        )
    for copy in asks + pieces:
        copy.start()
    for copy in asks:
        copy.wait()
    shard = place[0]
    core = lax.bitwise_and(shard, 1)

    def column(row):
        return jnp.broadcast_to(row, (128, 128)).T

    own_train = column(train[pl.ds(core, 1), :])
    other_train = column(train[pl.ds(1 - core, 1), :])
    asked = column(query[...])
    first = core == 0
    own_query = jnp.where(first, asked[:64], asked[64:])
    other_query = jnp.where(first, asked[64:], asked[:64])
    ids = jnp.concatenate([own_train, own_query, other_train, other_query], axis=0)
    ids = ids - shard * height
    lane = lax.broadcasted_iota(jnp.int32, ids.shape, 1)
    for start in range(0, height, 128):
        width = min(128, height - start)
        hit = jnp.where(ids == lane + start, 1.0, 0.0).astype(bf16)
        hot[:, start : start + width] = hit[:, :width]
    for j in range(LOOKUP_STEPS):
        pieces[j].wait()
        found = dot(hot[...], table[:, j * step : (j + 1) * step]).astype(bf16)
        mine[:, j * step : (j + 1) * step] = found[:192]
        other[:, j * step : (j + 1) * step] = found[192:]


def lookup(train_ids, query_ids, embed):
    height, wide = embed.shape
    out = shape((192, wide), bf16)
    return local_call(
        lookup_kernel,
        (out, out),
        lax.axis_index("shard").reshape(1),
        *in_hbm(train_ids.reshape(2, 128), query_ids.reshape(1, 128), embed),
        specs=[SMEM, HBM, HBM, HBM],
        vmem=24,
        scratch_shapes=[
            pltpu.VMEM((2, 128), jnp.int32),
            pltpu.VMEM((1, 128), jnp.int32),
            pltpu.VMEM((height, wide), bf16),
            pltpu.VMEM((384, height), bf16),
            pltpu.SemaphoreType.DMA((2 + LOOKUP_STEPS,)),
        ],
    )


def add_kernel(mine, got, out):
    for i in range(8):
        out[i] = mine[i] + got[i]


def norm_kernel(parts, gain, out):
    rows = parts[0]
    for i in range(1, 8):
        rows = rows + parts[i]
    rows = rows.astype(f32)
    inv_scale = lax.rsqrt(jnp.mean(rows * rows, axis=-1, keepdims=True) + norm_eps)
    normed = (rows * inv_scale * gain[...]).astype(bf16)
    for i in range(8):
        out[i] = normed


def acts_kernel(normed, w_gate, w_up, w_gate_other, w_up_other, out):
    rows = normed[...].T

    def product(w):
        return dot(w[...], rows)

    def hidden(gate_w, up_w):
        gate = product(gate_w)
        return (gate / (1.0 + jnp.exp(-gate))) * product(up_w)

    own = hidden(w_gate, w_up)
    other = hidden(w_gate_other, w_up_other)
    asked = jnp.concatenate([own[:, 128:], other[:, 128:]], axis=1)
    fill = jnp.zeros((PACK - 3 * UNITS, 128), f32)
    out[...] = jnp.concatenate([own[:, :128], other[:, :128], asked, fill], axis=0).astype(bf16)


def gather_groups(own, columns):
    def up(v):
        return lax.ppermute(v, "dp", z_shift(1))

    def down(v):
        return lax.ppermute(v, "dp", z_shift(-1))

    def across(v):
        return lax.ppermute(v, "dp", YLO)

    def together(*values):
        return lax.optimization_barrier(values)

    same, twin = {0: own}, {}
    twin[0], same[-1], same[1] = across(own), up(own), down(own)
    twin[1], same[-2], same[2] = across(same[1]), up(same[-1]), down(same[1])
    twin[2], twin[-1], same[-3], same[3] = across(same[2]), up(twin[0]), up(same[-2]), down(same[2])
    twin[3], twin[-2], same[4] = across(same[3]), up(twin[-1]), down(same[3])
    twin[-3], twin[4] = across(same[-3]), down(twin[3])
    return [group[step] for step in STEPS for group in (same, twin)], columns


def rhs_kernel(scale, *refs):
    blocks, (me, columns, part, flip, acts) = refs[:16], refs[16:]
    y = lax.shift_right_logical(me[0], 3)
    z = lax.bitwise_and(me[0], 7)
    empty = jnp.zeros((64, 128), bf16)
    out = jnp.zeros((PACK - BOTH, 256), f32)
    for i, step in enumerate(STEPS):
        pieces = []
        for side in (y, 1 - y):
            seen = columns[side * 8 + lax.bitwise_and(z + step, 7)]
            pieces.append(jnp.concatenate([seen, empty], axis=1))
            pieces.append(jnp.concatenate([empty, seen], axis=1))
        pair = blocks[2 * i], blocks[2 * i + 1]
        asked = jnp.concatenate([block[BOTH:, :] for block in pair], axis=1)
        out = out + dot(asked, jnp.concatenate(pieces, axis=0))
        for j, block in enumerate(pair):
            acts[:, (2 * i + j) * 128 : (2 * i + j + 1) * 128] = block[:BOTH, :]
    out = out * scale
    part[:UNITS] = out[:UNITS, :128].astype(bf16).astype(f32)
    part[UNITS:] = out[:UNITS, 128:].astype(bf16).astype(f32)
    flip[...] = jnp.concatenate([out[:UNITS, 128:], out[:UNITS, :128]], axis=0).astype(bf16)


def spread_tangent(res, acts, tangent):
    res_t = res.T.astype(bf16)
    for i in range(8):
        tangent[i] = dot(res_t, acts[:, i * 256 : (i + 1) * 256]).astype(bf16)


def first_kernel(acts, part, got, res_out, sums, tangent):
    res = part[...] + got[...].astype(f32)
    res_out[...] = res
    sums[...] = lanes([total(res * res)], (8, 128))
    spread_tangent(res, acts, tangent)


def share_kernel(parts, sums, *refs):
    earlier, (block_out, message) = refs[:-2], refs[-2:]
    block = jnp.sum(parts[...].astype(f32), axis=0).astype(bf16)
    block_out[...] = block
    block = block.astype(f32)
    values = [sums[0:1, 0:1], total(block * block)]
    if earlier:
        values.append(total(block * earlier[0][...].astype(f32)))
    extra = lanes(values, (16, 256))
    hi = extra.astype(bf16).astype(f32)
    mid = (extra - hi).astype(bf16).astype(f32)
    low = extra - hi - mid
    row = lax.broadcasted_iota(jnp.int32, (16, 256), 0)
    first_row = jnp.where(row == 0, hi, 0.0)
    mid = jnp.broadcast_to(mid[0:1], (16, 256))
    low = jnp.broadcast_to(low[0:1], (16, 256))
    extra = jnp.where(row == 1, mid, jnp.where(row == 2, low, first_row))
    whole = jnp.concatenate([block, extra], axis=0).astype(bf16)
    for i in range(8):
        message[i] = whole


def curve_kernel(acts, got, *refs):
    if len(refs) == 4:
        tangent_out, part, flip, sums_out = refs
    else:
        past, state, part, flip, sums_out = refs
    extra = got[0, 128:144, :].astype(f32)
    for i in range(1, 8):
        extra = extra + got[i, 128:144, :].astype(f32)
    sums = jnp.sum(extra, axis=0, keepdims=True)[:, :128]
    if len(refs) == 5:
        beta = guarded(sums[:, 0:1], state[0:1, 1:2])
    out = jnp.zeros((BOTH, 128), f32)
    for i in range(8):
        tangent = got[i, :128, :]
        if len(refs) == 4:
            tangent_out[i] = tangent
        else:
            tangent = (tangent.astype(f32) + beta * past[i].astype(f32)).astype(bf16)
        out = out + lax.dot_general(
            acts[:, i * 256 : (i + 1) * 256],
            tangent,
            (((1,), (1,)), ((), ())),
            preferred_element_type=f32,
        )
    row = lax.broadcasted_iota(jnp.int32, (8, 128), 0)
    sums = jnp.where(row == 0, jnp.broadcast_to(sums, (8, 128)), 0.0)
    sums_out[...] = sums
    part[...] = out.astype(bf16).astype(f32)
    flip[...] = jnp.concatenate([out[UNITS:], out[:UNITS]], axis=0).astype(bf16)


def second_kernel(acts, part, got, peer, sums, res, res_out, state, tangent):
    rr = sums[0:1, 0:1]
    tt = sums[0:1, 1:2] + peer[0:1, 1:2]
    inv_alpha = guarded(tt / TOKENS + damping * rr, rr)
    alpha = guarded(jnp.ones_like(inv_alpha), inv_alpha)
    old = res[...]
    new = old - alpha * ((part[...] + got[...].astype(f32)) / TOKENS + damping * old)
    res_out[...] = new
    state[...] = lanes([total(new * new), rr, tt, rr, inv_alpha], (8, 128))
    spread_tangent(new, acts, tangent)


def third_kernel(acts, part, got, peer, sums, past, res, res_before, res_out, state, tangent):
    rr = sums[0:1, 0:1]
    ww = sums[0:1, 1:2] + peer[0:1, 1:2]
    cross = sums[0:1, 2:3] + peer[0:1, 2:3]
    rr0, tt0, pp0, inv_alpha0 = (past[0:1, i : i + 1] for i in range(1, 5))
    beta = guarded(rr, rr0)
    tt = ww + 2.0 * beta * cross + beta * beta * tt0
    pp = rr + beta * beta * pp0
    inv_alpha = guarded(tt / TOKENS + damping * pp, rr)
    alpha = guarded(jnp.ones_like(inv_alpha), inv_alpha)
    old = res[...]
    direction = old + beta * res_before[...]
    new = old - alpha * ((part[...] + got[...].astype(f32)) / TOKENS + damping * direction)
    res_out[...] = new
    state[...] = lanes(
        [total(new * new), rr0, rr, tt, pp, inv_alpha0, inv_alpha, beta], (8, 128)
    )
    spread_tangent(new, acts, tangent)


def partial_kernel(parts, state, block0, block1, message):
    block2 = jnp.sum(parts[...].astype(f32), axis=0)
    beta = state[0:1, 7:8]
    step1 = block1[...].astype(f32) + beta * block0[...].astype(f32)
    out = lanes([0.5 * state[0:1, 0:1], total(block2 * block2), total(block2 * step1)], (1, 128))
    for i in range(16):
        message[i] = out


def group_kernel(got, state, message):
    sums = jnp.sum(got[...], axis=0)
    rr0, rr1, tt1, pp1, inv_alpha0, inv_alpha1, beta0 = (state[0:1, i : i + 1] for i in range(1, 8))
    rr2 = sums[:, 0:1]
    beta1 = guarded(rr2, rr1)
    tt2 = sums[:, 1:2] + 2.0 * beta1 * sums[:, 2:3] + beta1 * beta1 * tt1
    pp2 = rr2 + beta1 * beta1 * pp1
    inv_alpha2 = guarded(tt2 / TOKENS + damping * pp2, rr2)
    out = lanes([rr0, rr1, rr2, inv_alpha0, inv_alpha1, inv_alpha2, beta0, beta1], (1, 128))
    for i in range(16):
        message[i] = out


def whole_kernel(me, got, res0, res1, res2, out):
    every = jnp.concatenate([got[i] for i in range(16)], axis=0)
    n0, n1, n2, ia0, ia1, ia2, b0, b1 = (every[:, i : i + 1] for i in range(8))

    def apply_whole(u):
        u0, u1, u2 = u
        s0, s1, s2 = u0 - b0 * u1, u1 - b1 * u2, u2
        return s0 * ia0, s1 * ia1 - s0 * ia0, s2 * ia2 - s1 * ia1

    def inner(u, v):
        terms = u[0] * v[0] * n0 + u[1] * v[1] * n1 + u[2] * v[2] * n2
        return jnp.sum(terms, axis=0, keepdims=True)

    zero = jnp.zeros_like(n0)
    answer = (zero, zero, zero)
    res = (jnp.ones_like(n0), zero, zero)
    direction = res
    norm_now = inner(res, res)
    for turn in range(3):
        curved = apply_whole(direction)
        step = norm_now / inner(direction, curved)
        answer = tuple(a + step * d for a, d in zip(answer, direction))
        if turn < 2:
            res = tuple(r - step * c for r, c in zip(res, curved))
            norm_next = inner(res, res)
            ratio = norm_next / norm_now
            direction = tuple(r + ratio * d for r, d in zip(res, direction))
            norm_now = norm_next
    chosen = lax.broadcasted_iota(jnp.int32, n0.shape, 0) == me[0]
    mix = [jnp.sum(jnp.where(chosen, a, 0.0), axis=0, keepdims=True) for a in answer]
    out[...] = mix[0] * res0[:UNITS] + mix[1] * res1[:UNITS] + mix[2] * res2[:UNITS]


def body(train_ids, query_ids, embed, norm_gain, w_gate, w_up, cotangent):
    core = lax.axis_index("shard") % 2
    wide = embed.shape[1]
    w_gate, w_up = w_gate.T, w_up.T
    w_gate_other, w_up_other = swap_core(w_gate), swap_core(w_up)

    with jax.named_scope("rows"):
        mine, other = lookup(train_ids, query_ids, embed)
        other = swap_core(other).reshape(8, 24, wide)
        rows = local_call(
            add_kernel, pltpu.VMEM((8, 24, wide), bf16), mine.reshape(8, 24, wide), other
        )
        rows = exchange_chips(rows)
    with jax.named_scope("normed"):
        normed = local_call(
            norm_kernel, pltpu.VMEM((8, 24, wide), bf16), rows, norm_gain.reshape(1, wide)
        )
    with jax.named_scope("normed"):
        normed = exchange_chips(normed).reshape(192, wide)
    with jax.named_scope("acts"):
        package = local_call(
            acts_kernel, shape((PACK, 128), bf16), normed, w_gate, w_up, w_gate_other, w_up_other
        )
    with jax.named_scope("groups"):
        columns = lax.dynamic_slice_in_dim(cotangent, core * 64, 64, axis=0)
        columns = columns.reshape(64, 16, 128).transpose(1, 0, 2)
        columns, package = lax.optimization_barrier((columns, package))
        columns = lax.all_to_all(columns, "dp", 0, 0, tiled=True)
        blocks, columns = gather_groups(package, columns)
    vector = shape((BOTH, 128), f32)
    rounded = shape((BOTH, 128), bf16)
    small = shape((8, 128), f32)
    spread = shape((8, 128, 256), bf16)
    block = shape((128, 256), bf16)
    message = shape((8, 144, 256), bf16)
    table = shape((16, 1, 128), f32)

    with jax.named_scope("rhs"):
        part, flip, acts = local_call(
            functools.partial(rhs_kernel, 1.0 / math.sqrt(2048)),
            (vector, rounded, pltpu.VMEM((BOTH, TOKENS // 2), bf16)),
            *blocks,
            lax.axis_index("dp").reshape(1),
            columns,
            specs=[VMEM] * 16 + [SMEM, VMEM],
        )
        got = swap_core(flip)
    with jax.named_scope("first"):
        res0, sums, tangent = local_call(first_kernel, (vector, small, spread), acts, part, got)
        parts = exchange_chips(tangent)
        block0, shared = local_call(share_kernel, (block, message), parts, sums)
        shared = exchange_chips(shared)
        tangent0, part, flip, sums = local_call(
            curve_kernel, (spread, vector, rounded, small), acts, shared
        )
        got, peer = swap_core(flip), swap_core(sums)
    with jax.named_scope("second"):
        res1, state, tangent = local_call(
            second_kernel, (vector, small, spread), acts, part, got, peer, sums, res0
        )
        parts = exchange_chips(tangent)
        block1, shared = local_call(share_kernel, (block, message), parts, state, block0)
        shared = exchange_chips(shared)
        past = state
        part, flip, sums = local_call(
            curve_kernel, (vector, rounded, small), acts, shared, tangent0, state
        )
        got, peer = swap_core(flip), swap_core(sums)
    with jax.named_scope("third"):
        res2, state, tangent = local_call(
            third_kernel,
            (vector, small, spread),
            acts,
            part,
            got,
            peer,
            sums,
            past,
            res1,
            res0,
        )
        parts = exchange_chips(tangent)
        partials = local_call(partial_kernel, table, parts, state, block0, block1)
        partials = lax.all_to_all(partials, "shard", 0, 0, tiled=True)
    with jax.named_scope("whole"):
        mine = local_call(group_kernel, table, partials, state)
        every = lax.all_to_all(mine, "dp", 0, 0, tiled=True)
        return local_call(
            whole_kernel,
            shape((UNITS, 128), f32),
            lax.axis_index("dp").reshape(1),
            every,
            res0,
            res1,
            res2,
            specs=[SMEM] + [VMEM] * 4,
        )


def solution(mesh):
    placed = (
        P("dp"),
        P("dp"),
        P("shard", None),
        P(),
        P(None, "shard"),
        P(None, "shard"),
        P("dp", None),
    )
    return jax.shard_map(
        body, mesh=mesh, in_specs=placed, out_specs=P("shard", "dp"), check_vma=False
    )
```

```python
import functools
import math

import jax
import jax.numpy as jnp
from jax import lax
from jax.experimental import pallas as pl
from jax.experimental.pallas import tpu as pltpu
from jax.sharding import PartitionSpec as P

norm_eps = 1e-05
damping = 0.1

bf16 = jnp.bfloat16
f32 = jnp.float32

STEPS = (0, -1, 1, -2, 2, -3, 3, 4)
CHIPS = [[c + 2 * i for i in range(8)] for c in range(2)]
CORE = [(i, i ^ 1) for i in range(16)]
YLO = [(i, i ^ 8) for i in range(16)]
VMEM = pl.BlockSpec(memory_space=pltpu.VMEM)
SMEM = pl.BlockSpec(memory_space=pltpu.SMEM)
HBM = pl.BlockSpec(memory_space=pltpu.HBM)
UNITS = 344
BOTH = 2 * UNITS
PACK = 1040
TOKENS = 4096


def z_shift(step):
    return [(i, (i & 8) | ((i + step) & 7)) for i in range(16)]


def swap_core(v):
    return lax.ppermute(v, "shard", CORE)


def exchange_chips(v):
    return lax.all_to_all(v, "shard", 0, 0, axis_index_groups=CHIPS, tiled=True)


def local_call(kernel, outs, *args, specs=None, vmem=16, **more):
    return pl.pallas_call(
        kernel,
        out_shape=outs,
        in_specs=specs or [VMEM] * len(args),
        out_specs=jax.tree.map(lambda _: VMEM, outs),
        compiler_params=pltpu.CompilerParams(vmem_limit_bytes=vmem * 2**20),
        **more,
    )(*args)


def in_hbm(*values):
    return [pltpu.with_memory_space_constraint(v, pltpu.HBM) for v in values]


def shape(dims, dtype):
    return jax.ShapeDtypeStruct(dims, dtype)


def guarded(top, bottom):
    fine = bottom > 0
    return jnp.where(fine, top / jnp.where(fine, bottom, 1.0), 0.0)


def dot(a, b):
    return jnp.dot(a, b, preferred_element_type=f32)


def total(v):
    return jnp.sum(v, axis=(0, 1), keepdims=True)


def lanes(values, dims):
    lane = lax.broadcasted_iota(jnp.int32, dims, 1)
    row = lax.broadcasted_iota(jnp.int32, dims, 0)
    out = jnp.zeros(dims, f32)
    for i, v in enumerate(values):
        out = jnp.where((lane == i) & (row == 0), v, out)
    return out


LOOKUP_STEPS = 4


def lookup_kernel(place, train_hbm, query_hbm, table_hbm, mine, other, train, query, table, hot, sems):
    height, wide = table.shape
    step = wide // LOOKUP_STEPS
    asks = [
        pltpu.make_async_copy(train_hbm, train, sems.at[0]),
        pltpu.make_async_copy(query_hbm, query, sems.at[1]),
    ]
    pieces = []
    for j in range(LOOKUP_STEPS):
        span = pl.ds(j * step, step)
        pieces.append(
            pltpu.make_async_copy(table_hbm.at[:, span], table.at[:, span], sems.at[2 + j])
        )
    for copy in asks + pieces:
        copy.start()
    for copy in asks:
        copy.wait()
    shard = place[0]
    core = lax.bitwise_and(shard, 1)

    def column(row):
        return jnp.broadcast_to(row, (128, 128)).T

    own_train = column(train[pl.ds(core, 1), :])
    other_train = column(train[pl.ds(1 - core, 1), :])
    asked = column(query[...])
    first = core == 0
    own_query = jnp.where(first, asked[:64], asked[64:])
    other_query = jnp.where(first, asked[64:], asked[:64])
    ids = jnp.concatenate([own_train, own_query, other_train, other_query], axis=0)
    ids = ids - shard * height
    lane = lax.broadcasted_iota(jnp.int32, ids.shape, 1)
    for start in range(0, height, 128):
        width = min(128, height - start)
        hit = jnp.where(ids == lane + start, 1.0, 0.0).astype(bf16)
        hot[:, start : start + width] = hit[:, :width]
    for j in range(LOOKUP_STEPS):
        pieces[j].wait()
        found = dot(hot[...], table[:, j * step : (j + 1) * step]).astype(bf16)
        mine[:, j * step : (j + 1) * step] = found[:192]
        other[:, j * step : (j + 1) * step] = found[192:]


def lookup(train_ids, query_ids, embed):
    height, wide = embed.shape
    out = shape((192, wide), bf16)
    return local_call(
        lookup_kernel,
        (out, out),
        lax.axis_index("shard").reshape(1),
        *in_hbm(train_ids.reshape(2, 128), query_ids.reshape(1, 128), embed),
        specs=[SMEM, HBM, HBM, HBM],
        vmem=24,
        scratch_shapes=[
            pltpu.VMEM((2, 128), jnp.int32),
            pltpu.VMEM((1, 128), jnp.int32),
            pltpu.VMEM((height, wide), bf16),
            pltpu.VMEM((384, height), bf16),
            pltpu.SemaphoreType.DMA((2 + LOOKUP_STEPS,)),
        ],
    )


def add_kernel(mine, got, out):
    for i in range(8):
        out[i] = mine[i] + got[i]


def norm_kernel(parts, gain, out):
    rows = parts[0]
    for i in range(1, 8):
        rows = rows + parts[i]
    rows = rows.astype(f32)
    inv_scale = lax.rsqrt(jnp.mean(rows * rows, axis=-1, keepdims=True) + norm_eps)
    normed = (rows * inv_scale * gain[...]).astype(bf16)
    for i in range(8):
        out[i] = normed


def acts_kernel(normed, w_gate, w_up, w_gate_other, w_up_other, out):
    rows = normed[...].T

    def product(w):
        return dot(w[...], rows)

    def hidden(gate_w, up_w):
        gate = product(gate_w)
        return (gate / (1.0 + jnp.exp(-gate))) * product(up_w)

    own = hidden(w_gate, w_up)
    other = hidden(w_gate_other, w_up_other)
    asked = jnp.concatenate([own[:, 128:], other[:, 128:]], axis=1)
    fill = jnp.zeros((PACK - 3 * UNITS, 128), f32)
    out[...] = jnp.concatenate([own[:, :128], other[:, :128], asked, fill], axis=0).astype(bf16)


def deal_kernel(place, cotangent, *outs):
    y = lax.shift_right_logical(place[0], 3)
    z = lax.bitwise_and(place[0], 7)
    rows = pl.ds(pl.multiple_of(place[1] * 64, 64), 64)
    for step, out in zip(STEPS, outs):
        there = lax.bitwise_and(z - step, 7)
        for side in range(2):
            group = (1 - y if side else y) * 8 + there
            columns = pl.ds(pl.multiple_of(group * 128, 128), 128)
            out[side * 64 : (side + 1) * 64, :] = cotangent[rows, columns]


def pass_kernel(*refs):
    for i in range(8):
        refs[8][i * 64 : (i + 1) * 64, :] = refs[i][64:, :]


def gather_groups(own):
    def up(v):
        return lax.ppermute(v, "dp", z_shift(1))

    def down(v):
        return lax.ppermute(v, "dp", z_shift(-1))

    def across(v):
        return lax.ppermute(v, "dp", YLO)

    def together(*values):
        return lax.optimization_barrier(values)

    same, twin = {0: own}, {}
    twin[0], same[-1], same[1] = across(own), up(own), down(own)
    twin[1], same[-2], same[2] = across(same[1]), up(same[-1]), down(same[1])
    twin[2], twin[-1], same[-3], same[3] = across(same[2]), up(twin[0]), up(same[-2]), down(same[2])
    twin[3], twin[-2], same[4] = across(same[3]), up(twin[-1]), down(same[3])
    twin[-3], twin[4] = across(same[-3]), down(twin[3])
    return [group[step] for step in STEPS for group in (same, twin)]


def rhs_kernel(scale, *refs):
    blocks, columns, (part, flip, acts) = refs[:16], refs[16:25], refs[25:]
    empty = jnp.zeros((64, 128), bf16)
    out = jnp.zeros((PACK - BOTH, 256), f32)
    for i in range(8):
        pieces = []
        for side in range(2):
            seen = columns[8][i * 64 : (i + 1) * 64, :] if side else columns[i][:64, :]
            pieces.append(jnp.concatenate([seen, empty], axis=1))
            pieces.append(jnp.concatenate([empty, seen], axis=1))
        pair = blocks[2 * i], blocks[2 * i + 1]
        asked = jnp.concatenate([block[BOTH:, :] for block in pair], axis=1)
        out = out + dot(asked, jnp.concatenate(pieces, axis=0))
        for j, block in enumerate(pair):
            acts[:, (2 * i + j) * 128 : (2 * i + j + 1) * 128] = block[:BOTH, :]
    out = out * scale
    part[:UNITS] = out[:UNITS, :128]
    part[UNITS:] = out[:UNITS, 128:]
    flip[:UNITS] = out[:UNITS, 128:]
    flip[UNITS:] = out[:UNITS, :128]


def spread_tangent(res, acts, tangent):
    res_t = res.T.astype(bf16)
    for i in range(8):
        tangent[i] = dot(res_t, acts[:, i * 256 : (i + 1) * 256]).astype(bf16)


def first_kernel(acts, part, got, res_out, sums, tangent):
    res = part[...] + got[...]
    res_out[...] = res
    sums[...] = lanes([total(res * res)], (8, 128))
    spread_tangent(res, acts, tangent)


def share_kernel(parts, sums, *refs):
    earlier, (block_out, message) = refs[:-2], refs[-2:]
    block = jnp.sum(parts[...].astype(f32), axis=0).astype(bf16)
    block_out[...] = block
    block = block.astype(f32)
    values = [sums[0:1, 0:1], total(block * block)]
    if earlier:
        values.append(total(block * earlier[0][...].astype(f32)))
    extra = lanes(values, (16, 256))
    hi = extra.astype(bf16).astype(f32)
    mid = (extra - hi).astype(bf16).astype(f32)
    low = extra - hi - mid
    row = lax.broadcasted_iota(jnp.int32, (16, 256), 0)
    first_row = jnp.where(row == 0, hi, 0.0)
    mid = jnp.broadcast_to(mid[0:1], (16, 256))
    low = jnp.broadcast_to(low[0:1], (16, 256))
    extra = jnp.where(row == 1, mid, jnp.where(row == 2, low, first_row))
    whole = jnp.concatenate([block, extra], axis=0).astype(bf16)
    for i in range(8):
        message[i] = whole


def curve_kernel(acts, got, *refs):
    if len(refs) == 4:
        tangent_out, part, flip, sums_out = refs
    else:
        past, state, part, flip, sums_out = refs
    extra = got[0, 128:144, :].astype(f32)
    for i in range(1, 8):
        extra = extra + got[i, 128:144, :].astype(f32)
    sums = jnp.sum(extra, axis=0, keepdims=True)[:, :128]
    if len(refs) == 5:
        beta = guarded(sums[:, 0:1], state[0:1, 1:2])
    out = jnp.zeros((BOTH, 128), f32)
    for i in range(8):
        tangent = got[i, :128, :]
        if len(refs) == 4:
            tangent_out[i] = tangent
        else:
            tangent = (tangent.astype(f32) + beta * past[i].astype(f32)).astype(bf16)
        out = out + lax.dot_general(
            acts[:, i * 256 : (i + 1) * 256],
            tangent,
            (((1,), (1,)), ((), ())),
            preferred_element_type=f32,
        )
    row = lax.broadcasted_iota(jnp.int32, (8, 128), 0)
    sums = jnp.where(row == 0, jnp.broadcast_to(sums, (8, 128)), 0.0)
    sums_out[...] = sums
    part[...] = out
    flip[:UNITS] = out[UNITS:]
    flip[UNITS:BOTH] = out[:UNITS]
    flip[BOTH:] = sums


def second_kernel(acts, part, got, sums, res, res_out, state, tangent):
    rr = sums[0:1, 0:1]
    tt = sums[0:1, 1:2] + got[BOTH : BOTH + 1, 1:2]
    inv_alpha = guarded(tt / TOKENS + damping * rr, rr)
    alpha = guarded(jnp.ones_like(inv_alpha), inv_alpha)
    old = res[...]
    new = old - alpha * ((part[...] + got[:BOTH]) / TOKENS + damping * old)
    res_out[...] = new
    state[...] = lanes([total(new * new), rr, tt, rr, inv_alpha], (8, 128))
    spread_tangent(new, acts, tangent)


def third_kernel(acts, part, got, sums, past, res, res_before, res_out, state, tangent):
    rr = sums[0:1, 0:1]
    ww = sums[0:1, 1:2] + got[BOTH : BOTH + 1, 1:2]
    cross = sums[0:1, 2:3] + got[BOTH : BOTH + 1, 2:3]
    rr0, tt0, pp0, inv_alpha0 = (past[0:1, i : i + 1] for i in range(1, 5))
    beta = guarded(rr, rr0)
    tt = ww + 2.0 * beta * cross + beta * beta * tt0
    pp = rr + beta * beta * pp0
    inv_alpha = guarded(tt / TOKENS + damping * pp, rr)
    alpha = guarded(jnp.ones_like(inv_alpha), inv_alpha)
    old = res[...]
    direction = old + beta * res_before[...]
    new = old - alpha * ((part[...] + got[:BOTH]) / TOKENS + damping * direction)
    res_out[...] = new
    state[...] = lanes(
        [total(new * new), rr0, rr, tt, pp, inv_alpha0, inv_alpha, beta], (8, 128)
    )
    spread_tangent(new, acts, tangent)


def partial_kernel(parts, state, block0, block1, message):
    block2 = jnp.sum(parts[...].astype(f32), axis=0)
    beta = state[0:1, 7:8]
    step1 = block1[...].astype(f32) + beta * block0[...].astype(f32)
    out = lanes([0.5 * state[0:1, 0:1], total(block2 * block2), total(block2 * step1)], (1, 128))
    for i in range(16):
        message[i] = out


def group_kernel(got, state, message):
    sums = jnp.sum(got[...], axis=0)
    rr0, rr1, tt1, pp1, inv_alpha0, inv_alpha1, beta0 = (state[0:1, i : i + 1] for i in range(1, 8))
    rr2 = sums[:, 0:1]
    beta1 = guarded(rr2, rr1)
    tt2 = sums[:, 1:2] + 2.0 * beta1 * sums[:, 2:3] + beta1 * beta1 * tt1
    pp2 = rr2 + beta1 * beta1 * pp1
    inv_alpha2 = guarded(tt2 / TOKENS + damping * pp2, rr2)
    out = lanes([rr0, rr1, rr2, inv_alpha0, inv_alpha1, inv_alpha2, beta0, beta1], (1, 128))
    for i in range(16):
        message[i] = out


def whole_kernel(me, got, res0, res1, res2, out):
    every = jnp.concatenate([got[i] for i in range(16)], axis=0)
    n0, n1, n2, ia0, ia1, ia2, b0, b1 = (every[:, i : i + 1] for i in range(8))

    def apply_whole(u):
        u0, u1, u2 = u
        s0, s1, s2 = u0 - b0 * u1, u1 - b1 * u2, u2
        return s0 * ia0, s1 * ia1 - s0 * ia0, s2 * ia2 - s1 * ia1

    def inner(u, v):
        terms = u[0] * v[0] * n0 + u[1] * v[1] * n1 + u[2] * v[2] * n2
        return jnp.sum(terms, axis=0, keepdims=True)

    zero = jnp.zeros_like(n0)
    answer = (zero, zero, zero)
    res = (jnp.ones_like(n0), zero, zero)
    direction = res
    norm_now = inner(res, res)
    for turn in range(3):
        curved = apply_whole(direction)
        step = norm_now / inner(direction, curved)
        answer = tuple(a + step * d for a, d in zip(answer, direction))
        if turn < 2:
            res = tuple(r - step * c for r, c in zip(res, curved))
            norm_next = inner(res, res)
            ratio = norm_next / norm_now
            direction = tuple(r + ratio * d for r, d in zip(res, direction))
            norm_now = norm_next
    chosen = lax.broadcasted_iota(jnp.int32, n0.shape, 0) == me[0]
    mix = [jnp.sum(jnp.where(chosen, a, 0.0), axis=0, keepdims=True) for a in answer]
    out[...] = mix[0] * res0[:UNITS] + mix[1] * res1[:UNITS] + mix[2] * res2[:UNITS]


def body(train_ids, query_ids, embed, norm_gain, w_gate, w_up, cotangent):
    core = lax.axis_index("shard") % 2
    wide = embed.shape[1]
    w_gate, w_up = w_gate.T, w_up.T
    w_gate_other, w_up_other = swap_core(w_gate), swap_core(w_up)

    with jax.named_scope("rows"):
        mine, other = lookup(train_ids, query_ids, embed)
        other = swap_core(other).reshape(8, 24, wide)
        rows = local_call(
            add_kernel, pltpu.VMEM((8, 24, wide), bf16), mine.reshape(8, 24, wide), other
        )
        dealt = local_call(
            deal_kernel,
            (shape((128, 128), bf16),) * 8,
            jnp.stack([lax.axis_index("dp"), core]),
            cotangent,
            specs=[SMEM, VMEM],
        )
        rows, *dealt = lax.optimization_barrier((rows, *dealt))
        rows = exchange_chips(rows)
        columns = [dealt[0]] + [
            lax.ppermute(v, "dp", z_shift(-step)) for step, v in zip(STEPS[1:5], dealt[1:5])
        ]
        rows, *columns = lax.optimization_barrier((rows, *columns))
    with jax.named_scope("normed"):
        normed = local_call(
            norm_kernel, pltpu.VMEM((8, 24, wide), bf16), rows, norm_gain.reshape(1, wide)
        )
    with jax.named_scope("normed"):
        normed, *dealt = lax.optimization_barrier((normed, *dealt[5:]))
        normed = exchange_chips(normed).reshape(192, wide)
        columns += [lax.ppermute(v, "dp", z_shift(-step)) for step, v in zip(STEPS[5:], dealt)]
        normed, *columns = lax.optimization_barrier((normed, *columns))
        passed = local_call(pass_kernel, shape((512, 128), bf16), *columns)
        columns.append(lax.ppermute(passed, "dp", YLO))
    with jax.named_scope("acts"):
        package = local_call(
            acts_kernel, shape((PACK, 128), bf16), normed, w_gate, w_up, w_gate_other, w_up_other
        )
    with jax.named_scope("groups"):
        blocks = gather_groups(package)
    vector = shape((BOTH, 128), f32)
    longer = shape((BOTH + 8, 128), f32)
    small = shape((8, 128), f32)
    spread = shape((8, 128, 256), bf16)
    block = shape((128, 256), bf16)
    message = shape((8, 144, 256), bf16)
    table = shape((16, 1, 128), f32)

    with jax.named_scope("rhs"):
        part, flip, acts = local_call(
            functools.partial(rhs_kernel, 1.0 / math.sqrt(2048)),
            (vector, vector, pltpu.VMEM((BOTH, TOKENS // 2), bf16)),
            *blocks,
            *columns,
        )
        got = swap_core(flip)
    with jax.named_scope("first"):
        res0, sums, tangent = local_call(first_kernel, (vector, small, spread), acts, part, got)
        parts = exchange_chips(tangent)
        block0, shared = local_call(share_kernel, (block, message), parts, sums)
        shared = exchange_chips(shared)
        tangent0, part, flip, sums = local_call(
            curve_kernel, (spread, vector, longer, small), acts, shared
        )
        got = swap_core(flip)
    with jax.named_scope("second"):
        res1, state, tangent = local_call(
            second_kernel, (vector, small, spread), acts, part, got, sums, res0
        )
        parts = exchange_chips(tangent)
        block1, shared = local_call(share_kernel, (block, message), parts, state, block0)
        shared = exchange_chips(shared)
        past = state
        part, flip, sums = local_call(
            curve_kernel, (vector, longer, small), acts, shared, tangent0, state
        )
        got = swap_core(flip)
    with jax.named_scope("third"):
        res2, state, tangent = local_call(
            third_kernel,
            (vector, small, spread),
            acts,
            part,
            got,
            sums,
            past,
            res1,
            res0,
        )
        parts = exchange_chips(tangent)
        partials = local_call(partial_kernel, table, parts, state, block0, block1)
        partials = lax.all_to_all(partials, "shard", 0, 0, tiled=True)
    with jax.named_scope("whole"):
        mine = local_call(group_kernel, table, partials, state)
        every = lax.all_to_all(mine, "dp", 0, 0, tiled=True)
        return local_call(
            whole_kernel,
            shape((UNITS, 128), f32),
            lax.axis_index("dp").reshape(1),
            every,
            res0,
            res1,
            res2,
            specs=[SMEM] + [VMEM] * 4,
        )


def solution(mesh):
    placed = (
        P("dp"),
        P("dp"),
        P("shard", None),
        P(),
        P(None, "shard"),
        P(None, "shard"),
        P("dp", None),
    )
    return jax.shard_map(
        body, mesh=mesh, in_specs=placed, out_specs=P("shard", "dp"), check_vma=False
    )
```

```python
import functools
import math

import jax
import jax.numpy as jnp
from jax import lax
from jax.experimental import pallas as pl
from jax.experimental.pallas import tpu as pltpu
from jax.sharding import PartitionSpec as P

norm_eps = 1e-05
damping = 0.1

bf16 = jnp.bfloat16
f32 = jnp.float32

STEPS = (0, -1, 1, -2, 2, -3, 3, 4)
CHIPS = [[c + 2 * i for i in range(8)] for c in range(2)]
CORE = [(i, i ^ 1) for i in range(16)]
YLO = [(i, i ^ 8) for i in range(16)]
VMEM = pl.BlockSpec(memory_space=pltpu.VMEM)
SMEM = pl.BlockSpec(memory_space=pltpu.SMEM)
HBM = pl.BlockSpec(memory_space=pltpu.HBM)
UNITS = 344
BOTH = 2 * UNITS
PACK = 1040
TOKENS = 4096


def z_shift(step):
    return [(i, (i & 8) | ((i + step) & 7)) for i in range(16)]


def swap_core(v):
    return lax.ppermute(v, "shard", CORE)


def exchange_chips(v):
    return lax.all_to_all(v, "shard", 0, 0, axis_index_groups=CHIPS, tiled=True)


def local_call(kernel, outs, *args, specs=None, vmem=16, **more):
    return pl.pallas_call(
        kernel,
        out_shape=outs,
        in_specs=specs or [VMEM] * len(args),
        out_specs=jax.tree.map(lambda _: VMEM, outs),
        compiler_params=pltpu.CompilerParams(vmem_limit_bytes=vmem * 2**20),
        **more,
    )(*args)


def in_hbm(*values):
    return [pltpu.with_memory_space_constraint(v, pltpu.HBM) for v in values]


def shape(dims, dtype):
    return jax.ShapeDtypeStruct(dims, dtype)


def guarded(top, bottom):
    fine = bottom > 0
    return jnp.where(fine, top / jnp.where(fine, bottom, 1.0), 0.0)


def dot(a, b):
    return jnp.dot(a, b, preferred_element_type=f32)


def total(v):
    return jnp.sum(v, axis=(0, 1), keepdims=True)


def lanes(values, dims):
    lane = lax.broadcasted_iota(jnp.int32, dims, 1)
    row = lax.broadcasted_iota(jnp.int32, dims, 0)
    out = jnp.zeros(dims, f32)
    for i, v in enumerate(values):
        out = jnp.where((lane == i) & (row == 0), v, out)
    return out


LOOKUP_STEPS = 4


def lookup_kernel(place, train_hbm, query_hbm, table_hbm, mine, other, train, query, table, hot, sems):
    height, wide = table.shape
    step = wide // LOOKUP_STEPS
    asks = [
        pltpu.make_async_copy(train_hbm, train, sems.at[0]),
        pltpu.make_async_copy(query_hbm, query, sems.at[1]),
    ]
    pieces = []
    for j in range(LOOKUP_STEPS):
        span = pl.ds(j * step, step)
        pieces.append(
            pltpu.make_async_copy(table_hbm.at[:, span], table.at[:, span], sems.at[2 + j])
        )
    for copy in asks + pieces:
        copy.start()
    for copy in asks:
        copy.wait()
    shard = place[0]
    core = lax.bitwise_and(shard, 1)

    def column(row):
        return jnp.broadcast_to(row, (128, 128)).T

    own_train = column(train[pl.ds(core, 1), :])
    other_train = column(train[pl.ds(1 - core, 1), :])
    asked = column(query[...])
    first = core == 0
    own_query = jnp.where(first, asked[:64], asked[64:])
    other_query = jnp.where(first, asked[64:], asked[:64])
    ids = jnp.concatenate([own_train, own_query, other_train, other_query], axis=0)
    ids = ids - shard * height
    lane = lax.broadcasted_iota(jnp.int32, ids.shape, 1)
    for start in range(0, height, 128):
        width = min(128, height - start)
        hit = jnp.where(ids == lane + start, 1.0, 0.0).astype(bf16)
        hot[:, start : start + width] = hit[:, :width]
    for j in range(LOOKUP_STEPS):
        pieces[j].wait()
        found = dot(hot[...], table[:, j * step : (j + 1) * step]).astype(bf16)
        mine[:, j * step : (j + 1) * step] = found[:192]
        other[:, j * step : (j + 1) * step] = found[192:]


def lookup(train_ids, query_ids, embed):
    height, wide = embed.shape
    out = shape((192, wide), bf16)
    return local_call(
        lookup_kernel,
        (out, out),
        lax.axis_index("shard").reshape(1),
        *in_hbm(train_ids.reshape(2, 128), query_ids.reshape(1, 128), embed),
        specs=[SMEM, HBM, HBM, HBM],
        vmem=24,
        scratch_shapes=[
            pltpu.VMEM((2, 128), jnp.int32),
            pltpu.VMEM((1, 128), jnp.int32),
            pltpu.VMEM((height, wide), bf16),
            pltpu.VMEM((384, height), bf16),
            pltpu.SemaphoreType.DMA((2 + LOOKUP_STEPS,)),
        ],
    )


def add_kernel(mine, got, out):
    for i in range(8):
        out[i] = mine[i] + got[i]


def norm_kernel(parts, gain, out):
    rows = parts[0]
    for i in range(1, 8):
        rows = rows + parts[i]
    rows = rows.astype(f32)
    inv_scale = lax.rsqrt(jnp.mean(rows * rows, axis=-1, keepdims=True) + norm_eps)
    normed = (rows * inv_scale * gain[...]).astype(bf16)
    for i in range(8):
        out[i] = normed


def acts_kernel(normed, w_gate, w_up, w_gate_other, w_up_other, out):
    rows = normed[...].T

    def product(w):
        return dot(w[...], rows)

    def hidden(gate_w, up_w):
        gate = product(gate_w)
        return (gate / (1.0 + jnp.exp(-gate))) * product(up_w)

    own = hidden(w_gate, w_up)
    other = hidden(w_gate_other, w_up_other)
    asked = jnp.concatenate([own[:, 128:], other[:, 128:]], axis=1)
    fill = jnp.zeros((PACK - 3 * UNITS, 128), f32)
    out[...] = jnp.concatenate([own[:, :128], other[:, :128], asked, fill], axis=0).astype(bf16)


def deal_kernel(place, cotangent, *outs):
    y = lax.shift_right_logical(place[0], 3)
    z = lax.bitwise_and(place[0], 7)
    rows = pl.ds(pl.multiple_of(place[1] * 64, 64), 64)
    for step, out in zip(STEPS, outs):
        there = lax.bitwise_and(z - step, 7)
        for side in range(2):
            group = (1 - y if side else y) * 8 + there
            columns = pl.ds(pl.multiple_of(group * 128, 128), 128)
            out[side * 64 : (side + 1) * 64, :] = cotangent[rows, columns]


def pass_kernel(*refs):
    for i in range(8):
        refs[8][i * 64 : (i + 1) * 64, :] = refs[i][64:, :]


def gather_groups(own):
    def up(v):
        return lax.ppermute(v, "dp", z_shift(1))

    def down(v):
        return lax.ppermute(v, "dp", z_shift(-1))

    def across(v):
        return lax.ppermute(v, "dp", YLO)

    def together(*values):
        return lax.optimization_barrier(values)

    same, twin = {0: own}, {}
    twin[0], same[-1], same[1] = across(own), up(own), down(own)
    twin[1], same[-2], same[2] = across(same[1]), up(same[-1]), down(same[1])
    twin[2], twin[-1], same[-3], same[3] = across(same[2]), up(twin[0]), up(same[-2]), down(same[2])
    twin[3], twin[-2], same[4] = across(same[3]), up(twin[-1]), down(same[3])
    twin[-3], twin[4] = across(same[-3]), down(twin[3])
    return [group[step] for step in STEPS for group in (same, twin)]


def rhs_kernel(scale, *refs):
    blocks, columns, (part, flip, acts) = refs[:16], refs[16:25], refs[25:]
    empty = jnp.zeros((64, 128), bf16)
    out = jnp.zeros((PACK - BOTH, 256), f32)
    for i in range(8):
        pieces = []
        for side in range(2):
            seen = columns[8][i * 64 : (i + 1) * 64, :] if side else columns[i][:64, :]
            pieces.append(jnp.concatenate([seen, empty], axis=1))
            pieces.append(jnp.concatenate([empty, seen], axis=1))
        pair = blocks[2 * i], blocks[2 * i + 1]
        asked = jnp.concatenate([block[BOTH:, :] for block in pair], axis=1)
        out = out + dot(asked, jnp.concatenate(pieces, axis=0))
        for j, block in enumerate(pair):
            acts[:, (2 * i + j) * 128 : (2 * i + j + 1) * 128] = block[:BOTH, :]
    out = out * scale
    part[:UNITS] = out[:UNITS, :128]
    part[UNITS:] = out[:UNITS, 128:]
    flip[:UNITS] = out[:UNITS, 128:]
    flip[UNITS:] = out[:UNITS, :128]


def spread_tangent(res, acts, tangent):
    res_t = res.T.astype(bf16)
    for i in range(8):
        tangent[i] = dot(res_t, acts[:, i * 256 : (i + 1) * 256]).astype(bf16)


def first_kernel(acts, part, got, res_out, sums, tangent):
    res = part[...] + got[...]
    res_out[...] = res
    sums[...] = lanes([total(res * res)], (8, 128))
    spread_tangent(res, acts, tangent)


def share_kernel(parts, sums, *refs):
    earlier, (block_out, message) = refs[:-2], refs[-2:]
    block = jnp.sum(parts[...].astype(f32), axis=0).astype(bf16)
    block_out[...] = block
    block = block.astype(f32)
    values = [sums[0:1, 0:1], total(block * block)]
    if earlier:
        values.append(total(block * earlier[0][...].astype(f32)))
    extra = lanes(values, (16, 256))
    hi = extra.astype(bf16).astype(f32)
    mid = (extra - hi).astype(bf16).astype(f32)
    low = extra - hi - mid
    row = lax.broadcasted_iota(jnp.int32, (16, 256), 0)
    first_row = jnp.where(row == 0, hi, 0.0)
    mid = jnp.broadcast_to(mid[0:1], (16, 256))
    low = jnp.broadcast_to(low[0:1], (16, 256))
    extra = jnp.where(row == 1, mid, jnp.where(row == 2, low, first_row))
    whole = jnp.concatenate([block, extra], axis=0).astype(bf16)
    for i in range(8):
        message[i] = whole


def curve_kernel(acts, got, *refs):
    if len(refs) == 4:
        tangent_out, part, flip, sums_out = refs
    else:
        past, state, part, flip, sums_out = refs
    extra = got[0, 128:144, :].astype(f32)
    for i in range(1, 8):
        extra = extra + got[i, 128:144, :].astype(f32)
    sums = jnp.sum(extra, axis=0, keepdims=True)[:, :128]
    if len(refs) == 5:
        beta = guarded(sums[:, 0:1], state[0:1, 1:2])
    out = jnp.zeros((BOTH, 128), f32)
    for i in range(8):
        tangent = got[i, :128, :]
        if len(refs) == 4:
            tangent_out[i] = tangent
        else:
            tangent = (tangent.astype(f32) + beta * past[i].astype(f32)).astype(bf16)
        out = out + lax.dot_general(
            acts[:, i * 256 : (i + 1) * 256],
            tangent,
            (((1,), (1,)), ((), ())),
            preferred_element_type=f32,
        )
    row = lax.broadcasted_iota(jnp.int32, (8, 128), 0)
    sums = jnp.where(row == 0, jnp.broadcast_to(sums, (8, 128)), 0.0)
    sums_out[...] = sums
    part[...] = out
    flip[:UNITS] = out[UNITS:]
    flip[UNITS:BOTH] = out[:UNITS]
    flip[BOTH:] = sums


def second_kernel(acts, part, got, sums, res, res_out, state, tangent):
    rr = sums[0:1, 0:1]
    tt = sums[0:1, 1:2] + got[BOTH : BOTH + 1, 1:2]
    inv_alpha = guarded(tt / TOKENS + damping * rr, rr)
    alpha = guarded(jnp.ones_like(inv_alpha), inv_alpha)
    old = res[...]
    new = old - alpha * ((part[...] + got[:BOTH]) / TOKENS + damping * old)
    res_out[...] = new
    state[...] = lanes([total(new * new), rr, tt, rr, inv_alpha], (8, 128))
    spread_tangent(new, acts, tangent)


def third_kernel(acts, part, got, sums, past, res, res_before, res_out, state, tangent):
    rr = sums[0:1, 0:1]
    ww = sums[0:1, 1:2] + got[BOTH : BOTH + 1, 1:2]
    cross = sums[0:1, 2:3] + got[BOTH : BOTH + 1, 2:3]
    rr0, tt0, pp0, inv_alpha0 = (past[0:1, i : i + 1] for i in range(1, 5))
    beta = guarded(rr, rr0)
    tt = ww + 2.0 * beta * cross + beta * beta * tt0
    pp = rr + beta * beta * pp0
    inv_alpha = guarded(tt / TOKENS + damping * pp, rr)
    alpha = guarded(jnp.ones_like(inv_alpha), inv_alpha)
    old = res[...]
    direction = old + beta * res_before[...]
    new = old - alpha * ((part[...] + got[:BOTH]) / TOKENS + damping * direction)
    res_out[...] = new
    state[...] = lanes(
        [total(new * new), rr0, rr, tt, pp, inv_alpha0, inv_alpha, beta], (8, 128)
    )
    spread_tangent(new, acts, tangent)


def partial_kernel(parts, state, block0, block1, message):
    block2 = jnp.sum(parts[...].astype(f32), axis=0)
    beta = state[0:1, 7:8]
    step1 = block1[...].astype(f32) + beta * block0[...].astype(f32)
    out = lanes([0.5 * state[0:1, 0:1], total(block2 * block2), total(block2 * step1)], (1, 128))
    for i in range(16):
        message[i] = out


def group_kernel(got, state, message):
    sums = jnp.sum(got[...], axis=0)
    rr0, rr1, tt1, pp1, inv_alpha0, inv_alpha1, beta0 = (state[0:1, i : i + 1] for i in range(1, 8))
    rr2 = sums[:, 0:1]
    beta1 = guarded(rr2, rr1)
    tt2 = sums[:, 1:2] + 2.0 * beta1 * sums[:, 2:3] + beta1 * beta1 * tt1
    pp2 = rr2 + beta1 * beta1 * pp1
    inv_alpha2 = guarded(tt2 / TOKENS + damping * pp2, rr2)
    out = lanes([rr0, rr1, rr2, inv_alpha0, inv_alpha1, inv_alpha2, beta0, beta1], (1, 128))
    for i in range(16):
        message[i] = out


def whole_kernel(me, got, res0, res1, res2, out):
    every = jnp.concatenate([got[i] for i in range(16)], axis=0)
    n0, n1, n2, ia0, ia1, ia2, b0, b1 = (every[:, i : i + 1] for i in range(8))

    def apply_whole(u):
        u0, u1, u2 = u
        s0, s1, s2 = u0 - b0 * u1, u1 - b1 * u2, u2
        return s0 * ia0, s1 * ia1 - s0 * ia0, s2 * ia2 - s1 * ia1

    def inner(u, v):
        terms = u[0] * v[0] * n0 + u[1] * v[1] * n1 + u[2] * v[2] * n2
        return jnp.sum(terms, axis=0, keepdims=True)

    zero = jnp.zeros_like(n0)
    answer = (zero, zero, zero)
    res = (jnp.ones_like(n0), zero, zero)
    direction = res
    norm_now = inner(res, res)
    for turn in range(3):
        curved = apply_whole(direction)
        step = norm_now / inner(direction, curved)
        answer = tuple(a + step * d for a, d in zip(answer, direction))
        if turn < 2:
            res = tuple(r - step * c for r, c in zip(res, curved))
            norm_next = inner(res, res)
            ratio = norm_next / norm_now
            direction = tuple(r + ratio * d for r, d in zip(res, direction))
            norm_now = norm_next
    chosen = lax.broadcasted_iota(jnp.int32, n0.shape, 0) == me[0]
    mix = [jnp.sum(jnp.where(chosen, a, 0.0), axis=0, keepdims=True) for a in answer]
    out[...] = mix[0] * res0[:UNITS] + mix[1] * res1[:UNITS] + mix[2] * res2[:UNITS]


def body(train_ids, query_ids, embed, norm_gain, w_gate, w_up, cotangent):
    core = lax.axis_index("shard") % 2
    wide = embed.shape[1]
    w_gate, w_up = w_gate.T, w_up.T
    w_gate_other, w_up_other = swap_core(w_gate), swap_core(w_up)

    with jax.named_scope("rows"):
        mine, other = lookup(train_ids, query_ids, embed)
        other = swap_core(other).reshape(8, 24, wide)
        rows = local_call(
            add_kernel, pltpu.VMEM((8, 24, wide), bf16), mine.reshape(8, 24, wide), other
        )
        rows, cotangent = lax.optimization_barrier((rows, cotangent))
        dealt = local_call(
            deal_kernel,
            (shape((128, 128), bf16),) * 8,
            jnp.stack([lax.axis_index("dp"), core]),
            cotangent,
            specs=[SMEM, VMEM],
        )
        rows = exchange_chips(rows)
        columns = [dealt[0]] + [
            lax.ppermute(v, "dp", z_shift(-step)) for step, v in zip(STEPS[1:5], dealt[1:5])
        ]
        rows, *columns = lax.optimization_barrier((rows, *columns))
    with jax.named_scope("normed"):
        normed = local_call(
            norm_kernel, pltpu.VMEM((8, 24, wide), bf16), rows, norm_gain.reshape(1, wide)
        )
    with jax.named_scope("normed"):
        normed, *dealt = lax.optimization_barrier((normed, *dealt[5:]))
        normed = exchange_chips(normed).reshape(192, wide)
        columns += [lax.ppermute(v, "dp", z_shift(-step)) for step, v in zip(STEPS[5:], dealt)]
        passed = local_call(pass_kernel, shape((512, 128), bf16), *columns)
        columns.append(lax.ppermute(passed, "dp", YLO))
    with jax.named_scope("acts"):
        package = local_call(
            acts_kernel, shape((PACK, 128), bf16), normed, w_gate, w_up, w_gate_other, w_up_other
        )
    with jax.named_scope("groups"):
        blocks = gather_groups(package)
    vector = shape((BOTH, 128), f32)
    longer = shape((BOTH + 8, 128), f32)
    small = shape((8, 128), f32)
    spread = shape((8, 128, 256), bf16)
    block = shape((128, 256), bf16)
    message = shape((8, 144, 256), bf16)
    table = shape((16, 1, 128), f32)

    with jax.named_scope("rhs"):
        part, flip, acts = local_call(
            functools.partial(rhs_kernel, 1.0 / math.sqrt(2048)),
            (vector, vector, pltpu.VMEM((BOTH, TOKENS // 2), bf16)),
            *blocks,
            *columns,
        )
        got = swap_core(flip)
    with jax.named_scope("first"):
        res0, sums, tangent = local_call(first_kernel, (vector, small, spread), acts, part, got)
        parts = exchange_chips(tangent)
        block0, shared = local_call(share_kernel, (block, message), parts, sums)
        shared = exchange_chips(shared)
        tangent0, part, flip, sums = local_call(
            curve_kernel, (spread, vector, longer, small), acts, shared
        )
        got = swap_core(flip)
    with jax.named_scope("second"):
        res1, state, tangent = local_call(
            second_kernel, (vector, small, spread), acts, part, got, sums, res0
        )
        parts = exchange_chips(tangent)
        block1, shared = local_call(share_kernel, (block, message), parts, state, block0)
        shared = exchange_chips(shared)
        past = state
        part, flip, sums = local_call(
            curve_kernel, (vector, longer, small), acts, shared, tangent0, state
        )
        got = swap_core(flip)
    with jax.named_scope("third"):
        res2, state, tangent = local_call(
            third_kernel,
            (vector, small, spread),
            acts,
            part,
            got,
            sums,
            past,
            res1,
            res0,
        )
        parts = exchange_chips(tangent)
        partials = local_call(partial_kernel, table, parts, state, block0, block1)
        partials = lax.all_to_all(partials, "shard", 0, 0, tiled=True)
    with jax.named_scope("whole"):
        mine = local_call(group_kernel, table, partials, state)
        every = lax.all_to_all(mine, "dp", 0, 0, tiled=True)
        return local_call(
            whole_kernel,
            shape((UNITS, 128), f32),
            lax.axis_index("dp").reshape(1),
            every,
            res0,
            res1,
            res2,
            specs=[SMEM] + [VMEM] * 4,
        )


def solution(mesh):
    placed = (
        P("dp"),
        P("dp"),
        P("shard", None),
        P(),
        P(None, "shard"),
        P(None, "shard"),
        P("dp", None),
    )
    return jax.shard_map(
        body, mesh=mesh, in_specs=placed, out_specs=P("shard", "dp"), check_vma=False
    )
```
